32 devices in a mesh: blk: 16 (over z, y, x), pipe: 2 (over core).
Axes of the slice: x: 2, y: 2, z: 4, core: 2. Of those that a mesh axis runs over, the one named last changes fastest.
Arguments:
- x_saved: bfloat16 [2, 2, 2048, 4096], P('pipe', None, 'blk'), may hold values from -6 to 6
- cotangent: bfloat16 [2, 2048, 4096], P(None, 'blk'), may hold values from -6 to 6
- seq_right: bfloat16 [2, 16, 128, 128], P('pipe', 'blk'), may hold values from -0.5 to 0.5
- seq_left: bfloat16 [2, 128, 16, 16], P('pipe', 'blk'), may hold values from -1.5 to 1.5
- chan_first: bfloat16 [2, 64, 64, 64], P('pipe'), may hold values from -0.75 to 0.75
- chan_second: bfloat16 [2, 64, 64, 64], P('pipe'), may hold values from -0.75 to 0.75
Outputs:
- grad_input: bfloat16 [2, 2, 2048, 4096], P('pipe', None, 'blk')
- grad_right: float32 [2, 16, 128, 128], P('pipe', 'blk')
- grad_left: float32 [2, 128, 16, 16], P('pipe', 'blk')
- grad_first: float32 [2, 64, 64, 64], P('pipe')
- grad_second: float32 [2, 64, 64, 64], P('pipe')
The draws below stay inside these ranges and needn't reach their ends.
All inputs are finite; a program needn't handle non-finite values.
Results may differ from the reference program's by a relative error of at most 0.01.
Values may be sent and summed in bfloat16 or wider, within the bound.
No kernel may reach another device: no remote copies, remote signals or barrier semaphores. Data moves between devices by JAX's collectives and lax.ppermute only.
A program may use at most 128 MiB of HBM per device.

```python
import jax
import jax.numpy as jnp
from jax import lax

D = 4096
CB = 64
CNB = 64
SB = 128
NSB = 16
S = 2048
MB = 2
PIPES = 2


def level_of(stream_key, extent, shards, smallest, top_value):
    factor_of = 1.0
    for position, shards_of in shards:
        steps = jax.random.uniform(jax.random.fold_in(jax.random.fold_in(stream_key, 6), position), (shards_of,), jnp.float32, smallest / len(shards), top_value / len(shards))
        factor_of = factor_of * jnp.repeat(jnp.exp(steps), extent[position] // shards_of).reshape((-1,) + (1,) * (len(extent) - 1 - position))
    return factor_of


def centred(own_key, extent, deviation, reach, split=(), dtype=jnp.bfloat16):
    array = deviation * jax.random.normal(own_key, extent, jnp.float32)
    if split:
        array = array * level_of(own_key, extent, split, -0.22, 0.18)
    return jnp.clip(array, -reach, reach).astype(dtype)


def setup_inputs(seed: int = 0) -> dict:
    keys = jax.random.split(jax.random.key(seed), 7)
    x_saved = centred(keys[0], (PIPES, MB, S, D), 1.0, 6.0, ((0, 2), (2, 16)))
    cotangent = centred(keys[1], (MB, S, D), 1.0, 6.0, ((1, 16),))
    seq_right = centred(keys[2], (PIPES, NSB, SB, SB), SB ** -0.5, 0.5, ((0, 2), (1, 16)))
    seq_left = centred(keys[3], (PIPES, SB, NSB, NSB), NSB ** -0.5, 1.5, ((0, 2), (1, 16)))
    chan_first = centred(keys[4], (PIPES, CNB, CB, CB), CB ** -0.5, 0.75, ((0, 2),))
    chan_second = centred(keys[5], (PIPES, CB, CNB, CNB), CNB ** -0.5, 0.75, ((0, 2),))
    return dict(x_saved=x_saved, cotangent=cotangent, seq_right=seq_right, seq_left=seq_left, chan_first=chan_first, chan_second=chan_second)


def rounded(value):
    return lax.optimization_barrier(value.astype(jnp.bfloat16)).astype(jnp.float32)


def layer_backward(activation, grad_out, right_wide, left_wide, first_wide, second_wide):
    act_wide = activation.astype(jnp.float32)
    act_blocks = act_wide.reshape(S, CNB, CB)
    mixed = rounded(jnp.einsum('saj,akj->sak', act_blocks, first_wide))
    hidden = rounded(jnp.einsum('sak,kma->skm', mixed, second_wide))
    hidden_rows = hidden.reshape(NSB, SB, D)
    seq_rows = rounded(jnp.einsum('ikj,ijd->kid', right_wide, hidden_rows))
    carried = jnp.einsum('kmi,kid->kmd', left_wide, seq_rows).reshape(S, D)
    grad_wide = grad_out.astype(jnp.float32)
    gate_grad = rounded(grad_wide * act_wide).reshape(SB, NSB, D)
    left_grad = jnp.einsum('kmd,kid->kmi', gate_grad, seq_rows)
    back_rows = rounded(jnp.einsum('kmi,kmd->ikd', left_wide, gate_grad))
    right_grad = jnp.einsum('ikd,ijd->ikj', back_rows, hidden_rows)
    hidden_grad = rounded(jnp.einsum('ikj,ikd->ijd', right_wide, back_rows)).reshape(S, CB, CNB)
    second_grad = jnp.einsum('skm,sak->kma', hidden_grad, mixed)
    mixed_grad = rounded(jnp.einsum('skm,kma->sak', hidden_grad, second_wide))
    first_grad = jnp.einsum('sak,saj->akj', mixed_grad, act_blocks)
    chan_back = jnp.einsum('sak,akj->saj', mixed_grad, first_wide).reshape(S, D)
    input_grad = (grad_wide * carried + chan_back).astype(jnp.bfloat16)
    return input_grad, right_grad, left_grad, first_grad, second_grad


def reference(x_saved, cotangent, seq_right, seq_left, chan_first, chan_second):
    incoming = [cotangent[micro_index] for micro_index in range(MB)]
    grad_inputs = [None] * PIPES
    grad_rights = [None] * PIPES
    grad_lefts = [None] * PIPES
    grad_firsts = [None] * PIPES
    grad_seconds = [None] * PIPES
    for section in range(PIPES - 1, -1, -1):
        right_wide = seq_right[section].astype(jnp.float32)
        left_wide = seq_left[section].astype(jnp.float32)
        first_wide = chan_first[section].astype(jnp.float32)
        second_wide = chan_second[section].astype(jnp.float32)
        right_acc = jnp.zeros((NSB, SB, SB), jnp.float32)
        left_acc = jnp.zeros((SB, NSB, NSB), jnp.float32)
        first_acc = jnp.zeros((CNB, CB, CB), jnp.float32)
        second_acc = jnp.zeros((CB, CNB, CNB), jnp.float32)
        produced = []
        for micro_index in range(MB):
            result = layer_backward(x_saved[section, micro_index], incoming[micro_index],
                                    right_wide, left_wide, first_wide, second_wide)
            produced.append(result[0])
            right_acc = right_acc + result[1]
            left_acc = left_acc + result[2]
            first_acc = first_acc + result[3]
            second_acc = second_acc + result[4]
        incoming = produced
        grad_inputs[section] = jnp.stack(produced)
        grad_rights[section] = right_acc
        grad_lefts[section] = left_acc
        grad_firsts[section] = first_acc
        grad_seconds[section] = second_acc
    return (jnp.stack(grad_inputs), jnp.stack(grad_rights), jnp.stack(grad_lefts),
            jnp.stack(grad_firsts), jnp.stack(grad_seconds))
```

```python
import functools

import jax
import jax.numpy as jnp
from jax import lax
from jax.experimental import pallas as pl
from jax.experimental.pallas import tpu as pltpu
from jax.sharding import PartitionSpec as P

BF = jnp.bfloat16
F32 = jnp.float32
NN = (((1,), (0,)), ((), ()))
NT = (((1,), (1,)), ((), ()))


def mm(a, b, dims=NN):
    return lax.dot_general(a, b, dims, preferred_element_type=F32)


def whole(shape):
    return pl.BlockSpec(shape, lambda *_: (0,) * len(shape))


def call(kernel, name, out_shape, grid=None, in_specs=None, out_specs=None, scratch=(), prefetch=0, cost=None):
    params = pltpu.CompilerParams(vmem_limit_bytes=56 * 1024 * 1024)
    flops, moved = cost or (1 << 28, 8 << 20)
    estimate = pl.CostEstimate(flops=flops, bytes_accessed=moved, transcendentals=0)
    if grid is None:
        return pl.pallas_call(
            kernel, out_shape=out_shape, scratch_shapes=scratch, compiler_params=params, cost_estimate=estimate, name=name
        )
    spec = pltpu.PrefetchScalarGridSpec(
        num_scalar_prefetch=prefetch, grid=grid, in_specs=in_specs, out_specs=out_specs, scratch_shapes=scratch
    )
    return pl.pallas_call(
        kernel, out_shape=out_shape, grid_spec=spec, compiler_params=params, cost_estimate=estimate, name=name
    )


def sds(shape, dtype):
    return jax.ShapeDtypeStruct(shape, dtype)


def columns(q):
    return slice(128 * q, 128 * (q + 1))


def regroup(wide, q, blocks):
    parts = [wide[pl.ds(2 * q + h, blocks, stride=blocks), :] for h in range(2)]
    return jnp.concatenate(parts, axis=0).astype(BF)


def diagonal(product, side):
    lane = lax.broadcasted_iota(jnp.int32, (side, 2 * side), 1)
    return jnp.where(lane < side, product[:side], product[side:])


def expand_kernel(first, second, first_bd, first_bt, second_bd, second_bt):
    side = first.shape[1]
    zero = jnp.zeros((side, side), F32)
    for source, straight, turned in ((first, first_bd, first_bt), (second, second_bd, second_bt)):
        for q in range(source.shape[0] // 2):
            lower, upper = source[2 * q].astype(F32), source[2 * q + 1].astype(F32)
            block = jnp.concatenate(
                [jnp.concatenate([lower, zero], axis=1), jnp.concatenate([zero, upper], axis=1)], axis=0
            )
            straight[q] = block.astype(BF)
            turned[q] = block.T.astype(BF)


def gate_kernel(p, keep, recv, upstream, left_t, back):
    act = jnp.where(p[0] == 0, recv[...].astype(F32), keep[0].astype(F32))
    gate = (upstream[0].astype(F32) * act).astype(BF)
    back[...] = mm(left_t[...], gate).astype(BF)


def forward_kernel(act, right, first_bd, second_bd, eye, rows, mixed, right_act, wide):
    blocks = 64
    pairs = first_bd.shape[0]
    right_act[...] = mm(right[...], act[...]).astype(BF)
    for q in range(pairs):
        wide[columns(q), :] = mm(first_bd[q], right_act[:, columns(q)], NT)
    for q in range(pairs):
        pair = regroup(wide, q, blocks)
        mixed[columns(q), :] = pair
        hidden = mm(second_bd[q], pair).astype(BF)
        rows[:, columns(q)] = mm(eye[...], hidden, NT).astype(BF)


def right_kernel(act, right, out):
    out[...] = mm(right[...], act[...]).astype(BF)


def middle_kernel(
    back, second_bt, first_bt, mixed, right_act, right_t, act, chan_back, right_grad, grads, wide, turned
):
    blocks = 64
    pairs = first_bt.shape[0]
    for q in range(pairs):
        wide[columns(q), :] = mm(second_bt[q], back[:, columns(q)], NT)
        grads[1, 64 * q : 64 * (q + 1), :] = diagonal(mm(mixed[columns(q), :], back[:, columns(q)]), 64)
    for q in range(pairs):
        pair = regroup(wide, q, blocks)
        grads[0, 64 * q : 64 * (q + 1), :] = diagonal(mm(pair, right_act[:, columns(q)]), 64)
        piece = mm(first_bt[q], pair).astype(BF)
        turned[columns(q), :] = piece
        chan_back[:, columns(q)] = mm(right_t[...], piece, NT)
    right_grad[...] = mm(act[...], turned[...]).T


def turn_kernel(
    p,
    rows,
    upstream,
    act,
    chan_back,
    act_low,
    left,
    left_t_low,
    second_bt,
    first_bt,
    eye,
    input_grad,
    left_grad,
    gate_low,
    back_low,
    mixed_grad,
    sent,
    wide,
):
    step = pl.program_id(0)
    steps = pl.num_programs(0)
    pairs = second_bt.shape[0]
    gy = upstream[0].astype(F32)
    carried = mm(left[...], rows[...])
    incoming = (gy * carried + chan_back[...]).astype(BF)
    input_grad[...] = incoming
    gate = (gy * act[...].astype(F32)).astype(BF)
    term = mm(gate, rows[...], NT)

    @pl.when(step == 0)
    def _():
        left_grad[...] = term

    @pl.when(step > 0)
    def _():
        left_grad[...] += term

    gate = (incoming.astype(F32) * act_low[...].astype(F32)).astype(BF)
    gate_low[...] = gate
    back = mm(left_t_low[...], gate).astype(BF)
    back_low[...] = back
    for q in range(pairs):
        at = pl.multiple_of((step * pairs + q) * 128, 128)
        wide[pl.ds(at, 128), :] = mm(second_bt[q], back[:, columns(q)], NT)

    @pl.when(step == steps - 1)
    def _():
        for q in range(first_bt.shape[0]):
            pair = regroup(wide, q, 64)
            mixed_grad[columns(q), :] = pair
            piece = mm(first_bt[q], pair).astype(BF)
            sent[:, columns(q)] = mm(eye[...], piece, NT).astype(BF)


def lower_kernel(
    rows, first_bd, second_bd, left, gate, back, mixed_grad, carried, left_grad, grads, wide, turned
):
    pairs = first_bd.shape[0]
    for q in range(pairs):
        wide[columns(q), :] = mm(first_bd[q], rows[:, columns(q)], NT)
        grads[0, 64 * q : 64 * (q + 1), :] = diagonal(mm(mixed_grad[columns(q), :], rows[:, columns(q)]), 64)
    for q in range(pairs):
        pair = regroup(wide, q, 64)
        grads[1, 64 * q : 64 * (q + 1), :] = diagonal(mm(pair, back[:, columns(q)]), 64)
        hidden = mm(second_bd[q], pair).astype(BF)
        turned[columns(q), :] = hidden
        carried[:, columns(q)] = mm(left[...], hidden, NT)
    left_grad[...] = mm(gate[...], turned[...])


def last_kernel(received, right_t, upstream, carried, act, input_grad, right_grad):
    step = pl.program_id(0)
    chan_back = mm(right_t[...], received[...])
    input_grad[...] = (upstream[...].astype(F32) * carried[...] + chan_back).astype(BF)
    term = mm(received[...], act[...], NT)

    @pl.when(step == 0)
    def _():
        right_grad[...] = term

    @pl.when(step > 0)
    def _():
        right_grad[...] += term


def swap(value):
    return lax.ppermute(value, "pipe", [(0, 1), (1, 0)])


def exchange(rows, devices):
    chunks = rows.reshape(devices, rows.shape[0] // devices, *rows.shape[1:])
    return lax.all_to_all(chunks, "blk", split_axis=0, concat_axis=0, tiled=True).reshape(rows.shape)


def reduced(grads, core, devices):
    kept = lax.dynamic_index_in_dim(grads, core, 0, keepdims=False)
    sent = lax.dynamic_index_in_dim(grads, 1 - core, 0, keepdims=False)
    part = (kept + swap(sent)).astype(BF)
    rows = part.shape[0]
    pieces = exchange(part, devices).reshape(devices, rows // devices, 128)
    total = jnp.sum(pieces.astype(F32), axis=0).astype(BF)
    spread = jnp.broadcast_to(total[None], (devices,) + total.shape).reshape(rows, 128)
    return exchange(spread, devices)


def body(x_saved, cotangent, seq_right, seq_left, chan_first, chan_second):
    devices = lax.axis_size("blk")
    core = lax.axis_index("pipe")
    p = core.astype(jnp.int32).reshape(1)
    saved = x_saved[0]
    micro, tokens, width = saved.shape
    span = seq_right.shape[2]
    per, count = seq_left.shape[1], seq_left.shape[2]
    blocks, side = chan_first.shape[1], chan_first.shape[2]
    pairs = blocks // 2

    def by_section(own, other):
        return jnp.where(core == 0, own, other), jnp.where(core == 0, other, own)

    received = swap(lax.dynamic_index_in_dim(saved, 1 - core, 0, keepdims=False))
    left_0, left_1 = by_section(seq_left[0], swap(seq_left[0]))
    right_0, right_1 = by_section(seq_right[0, 0], swap(seq_right[0, 0]))
    first_0, first_1 = by_section(chan_first[0], swap(chan_first[0]))
    second_0, second_1 = by_section(chan_second[0], swap(chan_second[0]))
    own_act = lax.dynamic_index_in_dim(saved, core, 0, keepdims=False)
    act_0, act_1 = by_section(own_act, received)
    eye = jnp.eye(tokens, dtype=BF)

    def spread_left(block):
        apart = jnp.eye(per, dtype=BF)[:, None, None, :]
        full = (block[:, :, :, None] * apart).reshape(per * count, count * per)
        return full, full.T

    full_0, turned_0 = spread_left(left_0)
    full_1, turned_1 = spread_left(left_1)

    step = width // 8
    square = whole((tokens, tokens))
    moving = pl.BlockSpec((tokens, step), lambda i, *_: (0, i))
    chosen = pl.BlockSpec((1, tokens, step), lambda i, p: (p[0], 0, i))
    act_shape = (tokens, width)
    col_shape = (width, tokens)

    back_1 = call(
        gate_kernel,
        "gate",
        sds(act_shape, BF),
        grid=(width // step,),
        prefetch=1,
        in_specs=[chosen, moving, chosen, square],
        out_specs=moving,
    )(p, saved, received, cotangent, turned_1)
    returned_1 = exchange(back_1, devices)

    expanded = [sds((pairs, 2 * side, 2 * side), BF)] * 4
    expand = call(expand_kernel, "expand", expanded)
    fbd_1, fbt_1, sbd_1, sbt_1 = expand(first_1, second_1)
    fbd_0, fbt_0, sbd_0, sbt_0 = expand(first_0, second_0)

    rows_1, mixed_1, right_act_1 = call(
        forward_kernel,
        "forward",
        [sds(act_shape, BF), sds(col_shape, BF), sds(act_shape, BF)],
        scratch=[pltpu.VMEM(col_shape, F32)],
    )(act_1, right_1, fbd_1, sbd_1, eye)
    gathered_1 = exchange(rows_1, devices)

    right_act_0 = call(right_kernel, "right", sds(act_shape, BF))(act_0, right_0)
    gathered_0 = exchange(right_act_0, devices)

    chan_back_1, right_grad_1, grads_1 = call(
        middle_kernel,
        "middle",
        [sds(act_shape, F32), sds((span, span), F32), sds((2, pairs * side, 2 * side), F32)],
        scratch=[pltpu.VMEM(col_shape, F32), pltpu.VMEM(col_shape, BF)],
    )(returned_1, sbt_1, fbt_1, mixed_1, right_act_1, right_1.T, act_1)

    input_1, left_full_1, gate_0, back_0, mixed_grad_0, sent_0 = call(
        turn_kernel,
        "turn",
        [
            sds(act_shape, BF),
            sds((tokens, tokens), F32),
            sds(act_shape, BF),
            sds(act_shape, BF),
            sds(col_shape, BF),
            sds(act_shape, BF),
        ],
        grid=(width // step,),
        prefetch=1,
        in_specs=[
            moving,
            chosen,
            moving,
            moving,
            moving,
            square,
            square,
            pl.BlockSpec((step // (2 * side), 2 * side, 2 * side), lambda i, *_: (i, 0, 0)),
            whole((pairs, 2 * side, 2 * side)),
            square,
        ],
        out_specs=[moving, square, moving, moving, whole(col_shape), whole(act_shape)],
        scratch=[pltpu.VMEM(col_shape, F32)],
    )(p, gathered_1, cotangent, act_1, chan_back_1, act_0, full_1, turned_0, sbt_0, fbt_0, eye)
    returned_0 = exchange(sent_0, devices)

    carried_0, left_full_0, grads_0 = call(
        lower_kernel,
        "lower",
        [sds(act_shape, F32), sds((tokens, tokens), F32), sds((2, pairs * side, 2 * side), F32)],
        scratch=[pltpu.VMEM(col_shape, F32), pltpu.VMEM(col_shape, BF)],
    )(gathered_0, fbd_0, sbd_0, full_0, gate_0, back_0, mixed_grad_0)

    input_0, right_grad_0 = call(
        last_kernel,
        "last",
        [sds(act_shape, BF), sds((span, span), F32)],
        grid=(width // step,),
        in_specs=[moving, square, moving, moving, moving],
        out_specs=[moving, square],
    )(returned_0, right_0.T, input_1, carried_0, act_0)

    sums_1 = reduced(grads_1, core, devices)
    sums_0 = reduced(grads_0, core, devices)

    def left_blocks(full):
        apart = jnp.eye(per, dtype=F32)[:, None, None, :]
        return jnp.sum(full.reshape(per, count, count, per) * apart, axis=3)

    def to_sections(low, high):
        kept = jnp.where(core == 0, low, high)
        came = swap(jnp.where(core == 0, high, low))
        return jnp.where(core == 0, kept, came), jnp.where(core == 0, came, kept)

    input_grad = jnp.stack(to_sections(input_0, input_1))
    left_grad = sum(to_sections(left_blocks(left_full_0), left_blocks(left_full_1)))
    right_grad = sum(to_sections(right_grad_0, right_grad_1))
    first_sum, second_sum = to_sections(sums_0, sums_1)
    first_grad = first_sum.astype(F32).reshape(pairs, side, 2, side).transpose(0, 2, 1, 3).reshape(blocks, side, side)
    second_grad = second_sum.astype(F32).reshape(pairs, side, 2, side).transpose(0, 2, 3, 1).reshape(blocks, side, side)
    return (
        input_grad[None],
        right_grad[None, None],
        left_grad[None],
        first_grad[None],
        second_grad[None],
    )


def solution(mesh):
    in_specs = (
        P("pipe", None, "blk", None),
        P(None, "blk", None),
        P("pipe", "blk", None, None),
        P("pipe", "blk", None, None),
        P("pipe", None, None, None),
        P("pipe", None, None, None),
    )
    out_specs = (
        P("pipe", None, "blk", None),
        P("pipe", "blk", None, None),
        P("pipe", "blk", None, None),
        P("pipe", None, None, None),
        P("pipe", None, None, None),
    )
    return jax.shard_map(body, mesh=mesh, in_specs=in_specs, out_specs=out_specs, check_vma=False)
```

```python
import functools

import jax
import jax.numpy as jnp
import numpy as np
from jax import lax
from jax.experimental import pallas as pl
from jax.experimental.pallas import tpu as pltpu
from jax.sharding import PartitionSpec as P

BF = jnp.bfloat16
F32 = jnp.float32
NN = (((1,), (0,)), ((), ()))
NT = (((1,), (1,)), ((), ()))


def mm(a, b, dims=NN, precision=None):
    return lax.dot_general(a, b, dims, preferred_element_type=F32, precision=precision)


def whole(shape):
    return pl.BlockSpec(shape, lambda *_: (0,) * len(shape))


def call(kernel, name, out_shape, grid, in_specs, out_specs, scratch=()):
    params = pltpu.CompilerParams(vmem_limit_bytes=56 * 1024 * 1024)
    estimate = pl.CostEstimate(flops=1 << 28, bytes_accessed=8 << 20, transcendentals=0)
    spec = pltpu.PrefetchScalarGridSpec(
        num_scalar_prefetch=1, grid=grid, in_specs=in_specs, out_specs=out_specs, scratch_shapes=scratch
    )
    return pl.pallas_call(
        kernel, out_shape=out_shape, grid_spec=spec, compiler_params=params, cost_estimate=estimate, name=name
    )


def sds(shape, dtype):
    return jax.ShapeDtypeStruct(shape, dtype)


def columns(q):
    return slice(128 * q, 128 * (q + 1))


def half(q):
    return slice(64 * q, 64 * (q + 1))


def pick(p, low, high):
    return jnp.where(p[0] == 0, low.astype(F32), high.astype(F32))


def regroup(wide, q, blocks):
    parts = [wide[pl.ds(2 * q + h, blocks, stride=blocks), :] for h in range(2)]
    return jnp.concatenate(parts, axis=0).astype(BF)


def diagonal(product):
    lane = lax.broadcasted_iota(jnp.int32, (64, 128), 1)
    return jnp.where(lane < 64, product[:64], product[64:])


def spread(left, onehot, mask):
    return (mm(left, onehot, NT) * mask.astype(F32)).astype(BF)


def spread_turned(left, onehot, mask):
    return (mm(onehot, left, NT) * mask.astype(F32).T).astype(BF)


def gate_kernel(p, keep, recv, upstream, left_own, left_other, onehot, mask, back, left_t):
    @pl.when(pl.program_id(0) == 0)
    def _():
        left = pick(p, left_other[...], left_own[...]).astype(BF)
        left_t[...] = spread_turned(left, onehot[...], mask[...])

    act = pick(p, recv[...], keep[0])
    gate = (upstream[0].astype(F32) * act).astype(BF)
    back[...] = mm(left_t[...], gate).astype(BF)


def expand_kernel(section, p, first, first_other, second, second_other, first_bd, first_bt, second_bd, second_bt):
    side = first.shape[1]
    zero = jnp.zeros((side, side), F32)
    for own, other, straight, turned in (
        (first, first_other, first_bd, first_bt),
        (second, second_other, second_bd, second_bt),
    ):
        for q in range(own.shape[0] // 2):
            pair = [(own[2 * q + h], other[2 * q + h]) for h in range(2)]
            parts = [pick(p, b, a) if section else pick(p, a, b) for a, b in pair]
            block = jnp.concatenate(
                [jnp.concatenate([parts[0], zero], axis=1), jnp.concatenate([zero, parts[1]], axis=1)], axis=0
            )
            straight[q] = block.astype(BF)
            turned[q] = block.T.astype(BF)


def forward_kernel(
    p,
    keep,
    recv,
    right_own,
    right_other,
    first_bd,
    second_bd,
    eye,
    rows,
    mixed,
    right_act,
    act_0,
    act_1,
    right_t_1,
    right_t_0,
    right_0,
    wide,
):
    act_0[...] = pick(p, keep[0], recv[...]).astype(BF)
    act_1[...] = pick(p, recv[...], keep[0]).astype(BF)
    low = pick(p, right_own[...], right_other[...]).astype(BF)
    high = pick(p, right_other[...], right_own[...]).astype(BF)
    right_0[...] = low
    right_t_0[...] = low.astype(F32).T.astype(BF)
    right_t_1[...] = high.astype(F32).T.astype(BF)
    right_act[...] = mm(high, act_1[...]).astype(BF)
    pairs = first_bd.shape[0]
    for q in range(pairs):
        wide[columns(q), :] = mm(first_bd[q], right_act[:, columns(q)], NT)
    for q in range(pairs):
        pair = regroup(wide, q, 2 * pairs)
        mixed[columns(q), :] = pair
        hidden = mm(second_bd[q], pair).astype(BF)
        rows[:, columns(q)] = mm(eye[...], hidden, NT).astype(BF)


def middle_kernel(
    p,
    back,
    second_bt,
    first_bt,
    mixed,
    right_act,
    right_t,
    act,
    right_low,
    act_low,
    right_act_low,
    chan_back,
    right_grad,
    first_grad,
    second_grad,
    wide,
    turned,
):
    right_act_low[...] = mm(right_low[...], act_low[...]).astype(BF)
    pairs = first_bt.shape[0]
    for q in range(pairs):
        wide[columns(q), :] = mm(second_bt[q], back[:, columns(q)], NT)
        second_grad[half(q), :] = diagonal(mm(mixed[columns(q), :], back[:, columns(q)]).T).astype(BF)
    for q in range(pairs):
        pair = regroup(wide, q, 2 * pairs)
        first_grad[half(q), :] = diagonal(mm(pair, right_act[:, columns(q)])).astype(BF)
        piece = mm(first_bt[q], pair).astype(BF)
        turned[columns(q), :] = piece
        chan_back[:, columns(q)] = mm(right_t[...], piece, NT)
    right_grad[...] = mm(act[...], turned[...]).T


def turn_kernel(
    p,
    rows,
    upstream,
    act,
    chan_back,
    act_low,
    left_own,
    left_other,
    second_bt,
    first_bt,
    eye,
    onehot,
    mask,
    input_grad,
    left_grad,
    gate_low,
    back_low,
    mixed_grad,
    sent,
    wide,
    left_acc,
    left,
    left_t_low,
):
    step = pl.program_id(0)
    steps = pl.num_programs(0)
    pairs = second_bt.shape[0]

    @pl.when(step == 0)
    def _():
        left[...] = spread(pick(p, left_other[...], left_own[...]).astype(BF), onehot[...], mask[...])
        left_t_low[...] = spread_turned(pick(p, left_own[...], left_other[...]).astype(BF), onehot[...], mask[...])

    gy = upstream[0].astype(F32)
    carried = mm(left[...], rows[...])
    incoming = (gy * carried + chan_back[...]).astype(BF)
    input_grad[...] = incoming
    gate = (gy * act[...].astype(F32)).astype(BF)
    term = mm(gate, rows[...], NT)

    @pl.when(step == 0)
    def _():
        left_acc[...] = term

    @pl.when(step > 0)
    def _():
        left_acc[...] += term

    gate = (incoming.astype(F32) * act_low[...].astype(F32)).astype(BF)
    gate_low[...] = gate
    back = mm(left_t_low[...], gate).astype(BF)
    back_low[...] = back
    for q in range(pairs):
        at = pl.multiple_of((step * pairs + q) * 128, 128)
        wide[pl.ds(at, 128), :] = mm(second_bt[q], back[:, columns(q)], NT)

    @pl.when(step == steps - 1)
    def _():
        for q in range(first_bt.shape[0]):
            pair = regroup(wide, q, 2 * first_bt.shape[0])
            mixed_grad[columns(q), :] = pair
            piece = mm(first_bt[q], pair).astype(BF)
            sent[:, columns(q)] = mm(eye[...], piece, NT).astype(BF)
        left_grad[...] = mm(
            left_acc[...] * mask[...].astype(F32), onehot[...].astype(F32), precision=lax.Precision.HIGHEST
        )


def lower_kernel(
    p,
    rows,
    first_bd,
    second_bd,
    left_own,
    left_other,
    gate,
    back,
    mixed_grad,
    onehot,
    mask,
    carried,
    left_grad,
    first_grad,
    second_grad,
    wide,
    turned,
):
    pairs = first_bd.shape[0]
    left = spread(pick(p, left_own[...], left_other[...]).astype(BF), onehot[...], mask[...])
    for q in range(pairs):
        wide[columns(q), :] = mm(first_bd[q], rows[:, columns(q)], NT)
        first_grad[half(q), :] = diagonal(mm(mixed_grad[columns(q), :], rows[:, columns(q)])).astype(BF)
    for q in range(pairs):
        pair = regroup(wide, q, 2 * pairs)
        second_grad[half(q), :] = diagonal(mm(pair, back[:, columns(q)]).T).astype(BF)
        hidden = mm(second_bd[q], pair).astype(BF)
        turned[columns(q), :] = hidden
        carried[:, columns(q)] = mm(left, hidden, NT)
    term = mm(gate[...], turned[...])
    left_grad[...] = mm(term * mask[...].astype(F32), onehot[...].astype(F32), precision=lax.Precision.HIGHEST)


def last_kernel(p, received, right_t, upstream, carried, act, input_grad, right_grad):
    step = pl.program_id(0)
    chan_back = mm(right_t[...], received[...])
    input_grad[...] = (upstream[...].astype(F32) * carried[...] + chan_back).astype(BF)
    term = mm(received[...], act[...], NT)

    @pl.when(step == 0)
    def _():
        right_grad[...] = term

    @pl.when(step > 0)
    def _():
        right_grad[...] += term


def total_kernel(p, pieces, out):
    total = pieces[0].astype(F32)
    for i in range(1, pieces.shape[0]):
        total += pieces[i].astype(F32)
    out[...] = total.astype(BF)


def unpack_kernel(p, kept, came, first, second):
    side = first.shape[1]

    def unpack(array, out):
        for q in range(first.shape[0] // 2):
            parts = []
            for row in range(64 * q, 64 * (q + 1), min(64, array.shape[2])):
                owner, at = divmod(row, array.shape[2])
                parts.append(array[owner, 0, at : at + min(64, array.shape[2]), :].astype(F32))
            value = jnp.concatenate(parts, axis=0) if len(parts) > 1 else parts[0]
            out[2 * q] = value[:, :side]
            out[2 * q + 1] = value[:, side:]

    @pl.when(p[0] == 0)
    def _():
        unpack(kept, first)
        unpack(came, second)

    @pl.when(p[0] != 0)
    def _():
        unpack(kept, second)
        unpack(came, first)


def swap(value):
    return lax.ppermute(value, "pipe", [(0, 1), (1, 0)])


def after(value, *others):
    return lax.optimization_barrier((value, *others))[0]


def exchange(rows, devices):
    chunks = rows.reshape(devices, rows.shape[0] // devices, *rows.shape[1:])
    return lax.all_to_all(chunks, "blk", split_axis=0, concat_axis=0, tiled=True).reshape(rows.shape)


def body(x_saved, cotangent, seq_right, seq_left, chan_first, chan_second):
    devices = lax.axis_size("blk")
    core = lax.axis_index("pipe")
    p = core.astype(jnp.int32).reshape(1)
    saved = x_saved[0]
    micro, tokens, width = saved.shape
    span = seq_right.shape[2]
    per, count = seq_left.shape[1], seq_left.shape[2]
    blocks, side = chan_first.shape[1], chan_first.shape[2]
    pairs = blocks // 2

    received = swap(lax.dynamic_index_in_dim(saved, 1 - core, 0, keepdims=False))
    left_own = seq_left[0].reshape(per * count, count)
    left_other = swap(left_own)
    right_own = seq_right[0, 0]
    right_other = swap(right_own)
    first_own, first_other = chan_first[0], swap(chan_first[0])
    second_own, second_other = chan_second[0], swap(chan_second[0])

    place = np.arange(tokens)
    mask = jnp.asarray(place[:, None] // count == place[None, :] % per, BF)
    onehot = jnp.asarray(place[:, None] // per == np.arange(count)[None, :], BF)
    eye = jnp.asarray(np.eye(tokens), BF)

    step = width // 4
    square = whole((tokens, tokens))
    narrow = whole((tokens, count))
    moving = pl.BlockSpec((tokens, step), lambda i, *_: (0, i))
    chosen = pl.BlockSpec((1, tokens, step), lambda i, p: (p[0], 0, i))
    act_shape = (tokens, width)
    col_shape = (width, tokens)
    pair_shape = (pairs, 2 * side, 2 * side)
    grad_shape = (pairs * side, 2 * side)
    act_full, col_full, pair_full, grad_full = map(whole, (act_shape, col_shape, pair_shape, grad_shape))
    chosen_full = pl.BlockSpec((1,) + act_shape, lambda i, p: (p[0], 0, 0))
    box = whole((blocks, side, side))
    squared = sds((tokens, tokens), BF)

    back_1 = call(
        gate_kernel,
        "gate",
        sds(act_shape, BF),
        (width // step,),
        [chosen, moving, chosen, narrow, narrow, narrow, square],
        moving,
        [pltpu.VMEM((tokens, tokens), BF)],
    )(p, saved, received, cotangent, left_own, left_other, onehot, mask)
    returned_1 = exchange(back_1, devices)
    p = after(p, back_1)

    def expand(p, section):
        return call(
            functools.partial(expand_kernel, section),
            "expand",
            [sds(pair_shape, BF)] * 4,
            (1,),
            [box] * 4,
            [pair_full] * 4,
        )(p, first_own, first_other, second_own, second_other)

    fbd_1, fbt_1, sbd_1, sbt_1 = expand(p, 1)
    rows_1, mixed_1, right_act_1, act_0, act_1, right_t_1, right_t_0, right_0 = call(
        forward_kernel,
        "forward",
        [sds(act_shape, BF), sds(col_shape, BF)] + [sds(act_shape, BF)] * 3 + [squared] * 3,
        (1,),
        [chosen_full, act_full, square, square, pair_full, pair_full, square],
        [act_full, col_full] + [act_full] * 3 + [square] * 3,
        [pltpu.VMEM(col_shape, F32)],
    )(p, saved, received, right_own, right_other, fbd_1, sbd_1, eye)
    gathered_1 = exchange(rows_1, devices)
    p = after(p, rows_1)
    fbd_0, fbt_0, sbd_0, sbt_0 = expand(p, 0)

    right_act_0, chan_back_1, right_grad_1, first_1, second_1 = call(
        middle_kernel,
        "middle",
        [sds(act_shape, BF), sds(act_shape, F32), sds((span, span), F32)] + [sds(grad_shape, BF)] * 2,
        (1,),
        [act_full, pair_full, pair_full, col_full, act_full, square, act_full, square, act_full],
        [act_full, act_full, square, grad_full, grad_full],
        [pltpu.VMEM(col_shape, F32), pltpu.VMEM(col_shape, BF)],
    )(p, returned_1, sbt_1, fbt_1, mixed_1, right_act_1, right_t_1, act_1, right_0, act_0)
    gathered_0 = exchange(right_act_0, devices)

    def over_cores(first, second):
        came = swap(jnp.where(core == 0, second, first)).astype(F32)
        return (jnp.where(core == 0, first, second).astype(F32) + came).astype(BF)

    part_1 = over_cores(first_1, second_1)

    input_1, left_grad_1, gate_0, back_0, mixed_grad_0, sent_0 = call(
        turn_kernel,
        "turn",
        [
            sds(act_shape, BF),
            sds((tokens, count), F32),
            sds(act_shape, BF),
            sds(act_shape, BF),
            sds(col_shape, BF),
            sds(act_shape, BF),
        ],
        (width // step,),
        [
            moving,
            chosen,
            moving,
            moving,
            moving,
            narrow,
            narrow,
            pl.BlockSpec((step // (2 * side), 2 * side, 2 * side), lambda i, *_: (i, 0, 0)),
            pair_full,
            square,
            narrow,
            square,
        ],
        [moving, narrow, moving, moving, col_full, act_full],
        [pltpu.VMEM(col_shape, F32), pltpu.VMEM((tokens, tokens), F32)] + [pltpu.VMEM((tokens, tokens), BF)] * 2,
    )(
        p,
        gathered_1,
        cotangent,
        act_1,
        chan_back_1,
        act_0,
        left_own,
        left_other,
        sbt_0,
        fbt_0,
        eye,
        onehot,
        mask,
    )
    returned_0 = exchange(sent_0, devices)

    carried_0, left_grad_0, first_0, second_0 = call(
        lower_kernel,
        "lower",
        [sds(act_shape, F32), sds((tokens, count), F32)] + [sds(grad_shape, BF)] * 2,
        (1,),
        [act_full, pair_full, pair_full, narrow, narrow, act_full, act_full, col_full, narrow, square],
        [act_full, narrow, grad_full, grad_full],
        [pltpu.VMEM(col_shape, F32), pltpu.VMEM(col_shape, BF)],
    )(p, gathered_0, fbd_0, sbd_0, left_own, left_other, gate_0, back_0, mixed_grad_0, onehot, mask)

    parts = jnp.stack([over_cores(first_0, second_0), part_1]).reshape(2, devices, -1, 2 * side).swapaxes(0, 1)
    pieces = lax.all_to_all(after(parts, returned_0), "blk", split_axis=0, concat_axis=0, tiled=True)
    own = call(
        total_kernel, "total", sds(pieces.shape[1:], BF), (1,), [whole(pieces.shape)], whole(pieces.shape[1:])
    )(p, pieces)
    everyone = jnp.broadcast_to(own[None], (devices,) + own.shape)
    sums = lax.all_to_all(everyone, "blk", split_axis=0, concat_axis=0, tiled=True)
    sums_came = swap(lax.dynamic_slice_in_dim(sums, 1 - core, 1, axis=1))

    input_0, right_grad_0 = call(
        last_kernel,
        "last",
        [sds(act_shape, BF), sds((span, span), F32)],
        (width // step,),
        [moving, square, moving, moving, moving],
        [moving, square],
    )(p, returned_0, right_t_0, input_1, carried_0, act_0)

    def to_section(low, high):
        return jnp.where(core == 0, low, high) + swap(jnp.where(core == 0, high, low))

    came = swap(jnp.where(core == 0, input_1, input_0))
    input_grad = jnp.where(core == 0, jnp.stack([input_0, came]), jnp.stack([came, input_1]))
    left_grad = to_section(left_grad_0, left_grad_1).reshape(per, count, count)
    right_grad = to_section(right_grad_0, right_grad_1)
    p = after(p, input_grad, left_grad, right_grad)
    part = (sums.shape[0], 1) + sums.shape[2:]
    first_grad, second_grad = call(
        unpack_kernel,
        "unpack",
        [sds((blocks, side, side), F32)] * 2,
        (1,),
        [pl.BlockSpec(part, lambda i, p: (0, p[0], 0, 0)), whole(part)],
        [box] * 2,
    )(p, sums, sums_came)
    return (
        input_grad[None],
        right_grad[None, None],
        left_grad[None],
        first_grad[None],
        second_grad[None],
    )


def solution(mesh):
    in_specs = (
        P("pipe", None, "blk", None),
        P(None, "blk", None),
        P("pipe", "blk", None, None),
        P("pipe", "blk", None, None),
        P("pipe", None, None, None),
        P("pipe", None, None, None),
    )
    out_specs = (
        P("pipe", None, "blk", None),
        P("pipe", "blk", None, None),
        P("pipe", "blk", None, None),
        P("pipe", None, None, None),
        P("pipe", None, None, None),
    )
    return jax.shard_map(body, mesh=mesh, in_specs=in_specs, out_specs=out_specs, check_vma=False)
```

```python
import functools

import jax
import jax.numpy as jnp
import numpy as np
from jax import lax
from jax.experimental import pallas as pl
from jax.experimental.pallas import tpu as pltpu
from jax.sharding import PartitionSpec as P

BF = jnp.bfloat16
F32 = jnp.float32
NN = (((1,), (0,)), ((), ()))
NT = (((1,), (1,)), ((), ()))


def mm(a, b, dims=NN, precision=None):
    return lax.dot_general(a, b, dims, preferred_element_type=F32, precision=precision)


def whole(shape):
    return pl.BlockSpec(shape, lambda *_: (0,) * len(shape))


def call(kernel, name, out_shape, grid, in_specs, out_specs, scratch=(), scalars=0):
    params = pltpu.CompilerParams(vmem_limit_bytes=62 * 1024 * 1024)
    estimate = pl.CostEstimate(flops=1 << 28, bytes_accessed=8 << 20, transcendentals=0)
    spec = pltpu.PrefetchScalarGridSpec(
        num_scalar_prefetch=scalars, grid=grid, in_specs=in_specs, out_specs=out_specs, scratch_shapes=scratch
    )
    return pl.pallas_call(
        kernel, out_shape=out_shape, grid_spec=spec, compiler_params=params, cost_estimate=estimate, name=name
    )


def sds(shape, dtype):
    return jax.ShapeDtypeStruct(shape, dtype)


def columns(q):
    return slice(128 * q, 128 * (q + 1))


def half(q):
    return slice(64 * q, 64 * (q + 1))


def pick(p, low, high):
    return jnp.where(p[0] == 0, low.astype(F32), high.astype(F32))


def regroup(wide, q, blocks):
    parts = [wide[pl.ds(2 * q + h, blocks, stride=blocks), :] for h in range(2)]
    return jnp.concatenate(parts, axis=0).astype(BF)


def diagonal(product):
    lane = lax.broadcasted_iota(jnp.int32, (64, 128), 1)
    return jnp.where(lane < 64, product[:64], product[64:])


def store(grads, part, q, value):
    rows = grads.shape[2]
    piece = min(rows, 64)
    for first in range(0, 64, piece):
        owner, at = divmod(64 * q + first, rows)
        grads[owner, part, at : at + piece, :] = value[first : first + piece].astype(grads.dtype)


def spread(left, onehot, mask):
    return (mm(left, onehot, NT) * mask.astype(F32)).astype(BF)


def spread_turned(left, onehot, mask):
    return (mm(onehot, left, NT) * mask.astype(F32).T).astype(BF)


def gate_kernel(p, keep, recv, upstream, left_own, left_other, onehot, mask, back, left_t):
    @pl.when(pl.program_id(0) == 0)
    def _():
        left = pick(p, left_other[...], left_own[...]).astype(BF)
        left_t[...] = spread_turned(left, onehot[...], mask[...])

    act = pick(p, recv[...], keep[0])
    gate = (upstream[0].astype(F32) * act).astype(BF)
    back[...] = mm(left_t[...], gate).astype(BF)


def expand_kernel(section, p, first, first_other, second, second_other, first_bd, first_bt, second_bd, second_bt):
    side = first.shape[1]
    zero = jnp.zeros((side, side), F32)
    for own, other, straight, turned in (
        (first, first_other, first_bd, first_bt),
        (second, second_other, second_bd, second_bt),
    ):
        for q in range(own.shape[0] // 2):
            pair = [(own[2 * q + h], other[2 * q + h]) for h in range(2)]
            parts = [pick(p, b, a) if section else pick(p, a, b) for a, b in pair]
            block = jnp.concatenate(
                [jnp.concatenate([parts[0], zero], axis=1), jnp.concatenate([zero, parts[1]], axis=1)], axis=0
            )
            straight[q] = block.astype(BF)
            turned[q] = block.T.astype(BF)


def forward_kernel(
    p,
    keep,
    recv,
    right_own,
    right_other,
    upstream,
    left_own,
    left_other,
    onehot,
    mask,
    first_bd,
    second_bd,
    eye,
    rows,
    mixed,
    right_act,
    act_0,
    act_1,
    gate,
    right_t_1,
    right_t_0,
    right_0,
    full_1,
    full_0,
    turned_0,
    wide,
):
    act_0[...] = pick(p, keep[0], recv[...]).astype(BF)
    act = pick(p, recv[...], keep[0])
    act_1[...] = act.astype(BF)
    gate[...] = (upstream[0].astype(F32) * act).astype(BF)
    left_0 = pick(p, left_own[...], left_other[...]).astype(BF)
    left_1 = pick(p, left_other[...], left_own[...]).astype(BF)
    full_1[...] = spread(left_1, onehot[...], mask[...])
    full_0[...] = spread(left_0, onehot[...], mask[...])
    turned_0[...] = spread_turned(left_0, onehot[...], mask[...])
    low = pick(p, right_own[...], right_other[...]).astype(BF)
    high = pick(p, right_other[...], right_own[...]).astype(BF)
    right_0[...] = low
    right_t_0[...] = low.astype(F32).T.astype(BF)
    right_t_1[...] = high.astype(F32).T.astype(BF)
    right_act[...] = mm(high, act_1[...]).astype(BF)
    pairs = first_bd.shape[0]
    for q in range(pairs):
        wide[columns(q), :] = mm(first_bd[q], right_act[:, columns(q)], NT)
    for q in range(pairs):
        pair = regroup(wide, q, 2 * pairs)
        mixed[columns(q), :] = pair
        hidden = mm(second_bd[q], pair).astype(BF)
        rows[:, columns(q)] = mm(eye[...], hidden, NT).astype(BF)


def middle_kernel(
    back,
    second_bt,
    first_bt,
    mixed,
    right_act,
    right_t,
    act,
    right_low,
    act_low,
    right_act_low,
    chan_back,
    right_grad,
    grads,
    wide,
    turned,
):
    right_act_low[...] = mm(right_low[...], act_low[...]).astype(BF)
    pairs = first_bt.shape[0]
    for q in range(pairs):
        wide[columns(q), :] = mm(second_bt[q], back[:, columns(q)], NT)
        store(grads, 1, q, diagonal(mm(mixed[columns(q), :], back[:, columns(q)]).T))
    for q in range(pairs):
        pair = regroup(wide, q, 2 * pairs)
        store(grads, 0, q, diagonal(mm(pair, right_act[:, columns(q)])))
        piece = mm(first_bt[q], pair).astype(BF)
        turned[columns(q), :] = piece
        chan_back[:, columns(q)] = mm(right_t[...], piece, NT)
    right_grad[...] = mm(act[...], turned[...]).T


def turn_kernel(
    rows,
    upstream,
    gate_high,
    chan_back,
    act_low,
    left,
    left_t_low,
    second_bt,
    first_bt,
    eye,
    onehot,
    mask,
    input_grad,
    left_grad,
    gate_low,
    back_low,
    mixed_grad,
    sent,
    wide,
    left_acc,
):
    step = pl.program_id(0)
    steps = pl.num_programs(0)
    pairs = second_bt.shape[0]

    carried = mm(left[...], rows[...])
    incoming = (upstream[...].astype(F32) * carried + chan_back[...]).astype(BF)
    input_grad[...] = incoming
    term = mm(gate_high[...], rows[...], NT)

    @pl.when(step == 0)
    def _():
        left_acc[...] = term

    @pl.when(step > 0)
    def _():
        left_acc[...] += term

    gate = (incoming.astype(F32) * act_low[...].astype(F32)).astype(BF)
    gate_low[...] = gate
    back = mm(left_t_low[...], gate).astype(BF)
    back_low[...] = back
    for q in range(pairs):
        at = pl.multiple_of((step * pairs + q) * 128, 128)
        wide[pl.ds(at, 128), :] = mm(second_bt[q], back[:, columns(q)], NT)

    @pl.when(step == steps - 1)
    def _():
        for q in range(first_bt.shape[0]):
            pair = regroup(wide, q, 2 * first_bt.shape[0])
            mixed_grad[columns(q), :] = pair
            piece = mm(first_bt[q], pair).astype(BF)
            sent[:, columns(q)] = mm(eye[...], piece, NT).astype(BF)
        left_grad[...] = mm(
            left_acc[...] * mask[...].astype(F32), onehot[...].astype(F32), precision=lax.Precision.HIGHEST
        )


def lower_kernel(
    rows,
    first_bd,
    second_bd,
    left,
    gate,
    back,
    mixed_grad,
    onehot,
    mask,
    carried,
    left_grad,
    grads,
    wide,
    turned,
):
    pairs = first_bd.shape[0]
    for q in range(pairs):
        wide[columns(q), :] = mm(first_bd[q], rows[:, columns(q)], NT)
        store(grads, 0, q, diagonal(mm(mixed_grad[columns(q), :], rows[:, columns(q)])))
    for q in range(pairs):
        pair = regroup(wide, q, 2 * pairs)
        store(grads, 1, q, diagonal(mm(pair, back[:, columns(q)]).T))
        hidden = mm(second_bd[q], pair).astype(BF)
        turned[columns(q), :] = hidden
        carried[:, columns(q)] = mm(left[...], hidden, NT)
    term = mm(gate[...], turned[...])
    left_grad[...] = mm(term * mask[...].astype(F32), onehot[...].astype(F32), precision=lax.Precision.HIGHEST)


def last_kernel(received, right_t, upstream, carried, act, input_grad, right_grad):
    step = pl.program_id(0)
    chan_back = mm(right_t[...], received[...])
    input_grad[...] = (upstream[...].astype(F32) * carried[...] + chan_back).astype(BF)
    term = mm(received[...], act[...], NT)

    @pl.when(step == 0)
    def _():
        right_grad[...] = term

    @pl.when(step > 0)
    def _():
        right_grad[...] += term


def total_kernel(pieces, out):
    total = pieces[0].astype(F32)
    for i in range(1, pieces.shape[0]):
        total += pieces[i].astype(F32)
    out[...] = total.astype(BF)


def spread_kernel(*refs):
    total = sum(ref[...].astype(F32) for ref in refs[:-1]).astype(BF)
    for i in range(refs[-1].shape[0]):
        refs[-1][i] = total


def unpack_kernel(sums, first, second):
    side = first.shape[1]
    for part, out in enumerate((first, second)):
        block = sums[:, part].astype(F32).reshape(-1, 2 * side)
        for q in range(out.shape[0] // 2):
            out[2 * q] = block[half(q), :side]
            out[2 * q + 1] = block[half(q), side:]


def swap(value):
    return lax.ppermute(value, "pipe", [(0, 1), (1, 0)])


def after(value, *others):
    return lax.optimization_barrier((value, *others))[0]


def exchange(rows, devices):
    chunks = rows.reshape(devices, rows.shape[0] // devices, *rows.shape[1:])
    return lax.all_to_all(chunks, "blk", split_axis=0, concat_axis=0, tiled=True).reshape(rows.shape)


def summed(parts, devices):
    far = 12 if devices == 16 else 0
    members = devices // 2 if far else devices
    groups = [[member ^ f for member in range(members)] for f in ((0, far) if far else (0,))]
    shape = (members, devices // members * parts.shape[1]) + parts.shape[2:]

    def exchanged(value):
        return lax.all_to_all(value, "blk", split_axis=0, concat_axis=0, axis_index_groups=groups, tiled=True)

    pieces = exchanged(parts.reshape(shape))
    terms = [call(total_kernel, "total", sds(shape[1:], BF), (1,), [whole(shape)], whole(shape[1:]))(pieces)]
    if far:
        terms.append(lax.ppermute(terms[0], "blk", [(i, i ^ far) for i in range(devices)]))
    share = [whole(shape[1:])] * len(terms)
    return exchanged(call(spread_kernel, "spread", sds(shape, BF), (1,), share, whole(shape))(*terms)).reshape(parts.shape)


def body(x_saved, cotangent, seq_right, seq_left, chan_first, chan_second):
    devices = lax.axis_size("blk")
    core = lax.axis_index("pipe")
    p = core.astype(jnp.int32).reshape(1)
    saved = x_saved[0]
    micro, tokens, width = saved.shape
    span = seq_right.shape[2]
    per, count = seq_left.shape[1], seq_left.shape[2]
    blocks, side = chan_first.shape[1], chan_first.shape[2]
    pairs = blocks // 2

    received = swap(lax.dynamic_index_in_dim(saved, 1 - core, 0, keepdims=False))
    left_own = seq_left[0].reshape(per * count, count)
    left_other = swap(left_own)
    right_own = seq_right[0, 0]
    right_other = swap(right_own)
    first_own, first_other = chan_first[0], swap(chan_first[0])
    second_own, second_other = chan_second[0], swap(chan_second[0])

    place = np.arange(tokens)
    mask = jnp.asarray(place[:, None] // count == place[None, :] % per, BF)
    onehot = jnp.asarray(place[:, None] // per == np.arange(count)[None, :], BF)
    eye = jnp.asarray(np.eye(tokens), BF)

    step = width // 4
    square = whole((tokens, tokens))
    narrow = whole((tokens, count))
    moving = pl.BlockSpec((tokens, step), lambda i, *_: (0, i))
    chosen = pl.BlockSpec((1, tokens, step), lambda i, p: (p[0], 0, i))
    act_shape = (tokens, width)
    col_shape = (width, tokens)
    pair_shape = (pairs, 2 * side, 2 * side)
    owned = (devices, 2, pairs * side // devices, 2 * side)
    act_full, col_full, pair_full = map(whole, (act_shape, col_shape, pair_shape))
    chosen_full = pl.BlockSpec((1,) + act_shape, lambda i, p: (p[0], 0, 0))
    box = whole((blocks, side, side))
    squared = sds((tokens, tokens), BF)

    back_1 = call(
        gate_kernel,
        "gate",
        sds(act_shape, BF),
        (width // step,),
        [chosen, moving, chosen, narrow, narrow, narrow, square],
        moving,
        [pltpu.VMEM((tokens, tokens), BF)],
        scalars=1,
    )(p, saved, received, cotangent, left_own, left_other, onehot, mask)
    returned_1 = exchange(back_1, devices)
    p = after(p, back_1)

    def expand(p, section):
        return call(
            functools.partial(expand_kernel, section),
            "expand",
            [sds(pair_shape, BF)] * 4,
            (1,),
            [box] * 4,
            [pair_full] * 4,
            scalars=1,
        )(p, first_own, first_other, second_own, second_other)

    fbd_1, fbt_1, sbd_1, sbt_1 = expand(p, 1)
    rows_1, mixed_1, right_act_1, act_0, act_1, gate_1, right_t_1, right_t_0, right_0, full_1, full_0, turned_0 = call(
        forward_kernel,
        "forward",
        [sds(act_shape, BF), sds(col_shape, BF)] + [sds(act_shape, BF)] * 4 + [squared] * 6,
        (1,),
        [chosen_full, act_full, square, square, chosen_full, narrow, narrow, narrow, square, pair_full, pair_full, square],
        [act_full, col_full] + [act_full] * 4 + [square] * 6,
        [pltpu.VMEM(col_shape, F32)],
        scalars=1,
    )(
        p,
        saved,
        received,
        right_own,
        right_other,
        cotangent,
        left_own,
        left_other,
        onehot,
        mask,
        fbd_1,
        sbd_1,
        eye,
    )
    gathered_1 = exchange(rows_1, devices)
    p = after(p, rows_1)
    fbd_0, fbt_0, sbd_0, sbt_0 = expand(p, 0)

    right_act_0, chan_back_1, right_grad_1, grads_1 = call(
        middle_kernel,
        "middle",
        [sds(act_shape, BF), sds(act_shape, F32), sds((span, span), F32), sds(owned, BF)],
        (1,),
        [act_full, pair_full, pair_full, col_full, act_full, square, act_full, square, act_full],
        [act_full, act_full, square, whole(owned)],
        [pltpu.VMEM(col_shape, F32), pltpu.VMEM(col_shape, BF)],
    )(returned_1, sbt_1, fbt_1, mixed_1, right_act_1, right_t_1, act_1, right_0, act_0)
    gathered_0 = exchange(right_act_0, devices)

    input_1, left_grad_1, gate_0, back_0, mixed_grad_0, sent_0 = call(
        turn_kernel,
        "turn",
        [
            sds(act_shape, BF),
            sds((tokens, count), F32),
            sds(act_shape, BF),
            sds(act_shape, BF),
            sds(col_shape, BF),
            sds(act_shape, BF),
        ],
        (width // step,),
        [
            moving,
            moving,
            moving,
            moving,
            moving,
            square,
            square,
            pl.BlockSpec((step // (2 * side), 2 * side, 2 * side), lambda i: (i, 0, 0)),
            pair_full,
            square,
            narrow,
            square,
        ],
        [moving, narrow, moving, moving, col_full, act_full],
        [pltpu.VMEM(col_shape, F32), pltpu.VMEM((tokens, tokens), F32)],
    )(
        gathered_1,
        lax.dynamic_index_in_dim(cotangent, core, 0, keepdims=False),
        gate_1,
        chan_back_1,
        act_0,
        full_1,
        turned_0,
        sbt_0,
        fbt_0,
        eye,
        onehot,
        mask,
    )
    returned_0 = exchange(sent_0, devices)


    carried_0, left_grad_0, grads_0 = call(
        lower_kernel,
        "lower",
        [sds(act_shape, F32), sds((tokens, count), F32), sds(owned, BF)],
        (1,),
        [act_full, pair_full, pair_full, square, act_full, act_full, col_full, narrow, square],
        [act_full, narrow, whole(owned)],
        [pltpu.VMEM(col_shape, F32), pltpu.VMEM(col_shape, BF)],
    )(gathered_0, fbd_0, sbd_0, full_0, gate_0, back_0, mixed_grad_0, onehot, mask)

    own = jnp.where(core == 0, grads_0, grads_1).astype(F32)
    parts = (own + swap(jnp.where(core == 0, grads_1, grads_0)).astype(F32)).astype(BF)
    sums = summed(after(parts, returned_0), devices)

    input_0, right_grad_0 = call(
        last_kernel,
        "last",
        [sds(act_shape, BF), sds((span, span), F32)],
        (width // step,),
        [moving, square, moving, moving, moving],
        [moving, square],
    )(returned_0, right_t_0, input_1, carried_0, act_0)

    def to_section(low, high):
        return jnp.where(core == 0, low, high) + swap(jnp.where(core == 0, high, low))

    left_grad = to_section(left_grad_0, left_grad_1).reshape(per, count, count)
    right_grad = to_section(right_grad_0, right_grad_1)
    input_grad = jnp.where(
        core == 0, jnp.stack([input_0, swap(input_0)]), jnp.stack([swap(input_1), input_1])
    )
    parts = 4
    first_grad, second_grad = call(
        unpack_kernel,
        "unpack",
        [sds((blocks, side, side), F32)] * 2,
        (parts,),
        [pl.BlockSpec((devices // parts,) + owned[1:], lambda i: (i, 0, 0, 0))],
        [pl.BlockSpec((blocks // parts, side, side), lambda i: (i, 0, 0))] * 2,
    )(after(sums, input_grad, left_grad, right_grad))
    return (
        input_grad[None],
        right_grad[None, None],
        left_grad[None],
        first_grad[None],
        second_grad[None],
    )


def solution(mesh):
    in_specs = (
        P("pipe", None, "blk", None),
        P(None, "blk", None),
        P("pipe", "blk", None, None),
        P("pipe", "blk", None, None),
        P("pipe", None, None, None),
        P("pipe", None, None, None),
    )
    out_specs = (
        P("pipe", None, "blk", None),
        P("pipe", "blk", None, None),
        P("pipe", "blk", None, None),
        P("pipe", None, None, None),
        P("pipe", None, None, None),
    )
    return jax.shard_map(body, mesh=mesh, in_specs=in_specs, out_specs=out_specs, check_vma=False)
```

```python
import functools

import jax
import jax.numpy as jnp
import numpy as np
from jax import lax
from jax.experimental import pallas as pl
from jax.experimental.pallas import tpu as pltpu
from jax.sharding import PartitionSpec as P

BF = jnp.bfloat16
F32 = jnp.float32
NN = (((1,), (0,)), ((), ()))
NT = (((1,), (1,)), ((), ()))


def mm(a, b, dims=NN, precision=None):
    return lax.dot_general(a, b, dims, preferred_element_type=F32, precision=precision)


def whole(shape):
    return pl.BlockSpec(shape, lambda *_: (0,) * len(shape))


def call(kernel, name, out_shape, grid, in_specs, out_specs, scratch=(), scalars=0, room=62):
    params = pltpu.CompilerParams(vmem_limit_bytes=room * 1024 * 1024)
    estimate = pl.CostEstimate(flops=1 << 28, bytes_accessed=8 << 20, transcendentals=0)
    spec = pltpu.PrefetchScalarGridSpec(
        num_scalar_prefetch=scalars, grid=grid, in_specs=in_specs, out_specs=out_specs, scratch_shapes=scratch
    )
    return pl.pallas_call(
        kernel, out_shape=out_shape, grid_spec=spec, compiler_params=params, cost_estimate=estimate, name=name
    )


def sds(shape, dtype):
    return jax.ShapeDtypeStruct(shape, dtype)


def columns(q):
    return slice(128 * q, 128 * (q + 1))


def half(q):
    return slice(64 * q, 64 * (q + 1))


def pick(p, low, high):
    return jnp.where(p[0] == 0, low.astype(F32), high.astype(F32))


def regroup(wide, q, blocks):
    parts = [wide[pl.ds(2 * q + h, blocks, stride=blocks), :] for h in range(2)]
    return jnp.concatenate(parts, axis=0).astype(BF)


def diagonal(product):
    lane = lax.broadcasted_iota(jnp.int32, (64, 128), 1)
    return jnp.where(lane < 64, product[:64], product[64:])


def store(grads, part, q, value):
    rows = grads.shape[2]
    piece = min(rows, 64)
    for first in range(0, 64, piece):
        owner, at = divmod(64 * q + first, rows)
        grads[owner, part, at : at + piece, :] = value[first : first + piece].astype(grads.dtype)


def spread(left, onehot, mask):
    return (mm(left, onehot, NT) * mask.astype(F32)).astype(BF)


def spread_turned(left, onehot, mask):
    return (mm(onehot, left, NT) * mask.astype(F32).T).astype(BF)


def left_kernel(left, onehot, mask, full, turned):
    full[...] = spread(left[...], onehot[...], mask[...])
    turned[...] = spread_turned(left[...], onehot[...], mask[...])


def expand_kernel(section, p, first, first_other, second, second_other, first_bd, first_bt, second_bd, second_bt):
    side = first.shape[1]
    zero = jnp.zeros((side, side), F32)
    for own, other, straight, turned in (
        (first, first_other, first_bd, first_bt),
        (second, second_other, second_bd, second_bt),
    ):
        for q in range(own.shape[0] // 2):
            pair = [(own[2 * q + h], other[2 * q + h]) for h in range(2)]
            parts = [pick(p, b, a) if section else pick(p, a, b) for a, b in pair]
            block = jnp.concatenate(
                [jnp.concatenate([parts[0], zero], axis=1), jnp.concatenate([zero, parts[1]], axis=1)], axis=0
            )
            straight[q] = block.astype(BF)
            turned[q] = block.T.astype(BF)


def forward_kernel(
    p,
    act,
    right_own,
    right_other,
    first_bd,
    second_bd,
    eye,
    rows,
    mixed,
    right_act,
    right_t_1,
    right_t_0,
    right_0,
    wide,
):
    low = pick(p, right_own[...], right_other[...]).astype(BF)
    high = pick(p, right_other[...], right_own[...]).astype(BF)
    right_0[...] = low
    right_t_0[...] = low.astype(F32).T.astype(BF)
    right_t_1[...] = high.astype(F32).T.astype(BF)
    right_act[...] = mm(high, act[...]).astype(BF)
    pairs = first_bd.shape[0]
    for q in range(pairs):
        wide[columns(q), :] = mm(first_bd[q], right_act[:, columns(q)], NT)
    for q in range(pairs):
        pair = regroup(wide, q, 2 * pairs)
        mixed[columns(q), :] = pair
        hidden = mm(second_bd[q], pair).astype(BF)
        rows[:, columns(q)] = mm(eye[...], hidden, NT).astype(BF)


def middle_kernel(
    back,
    second_bt,
    first_bt,
    mixed,
    right_act,
    right_t,
    act,
    right_low,
    act_low,
    right_act_low,
    chan_back,
    right_grad,
    grads,
    wide,
    turned,
):
    right_act_low[...] = mm(right_low[...], act_low[...]).astype(BF)
    pairs = first_bt.shape[0]
    for q in range(pairs):
        wide[columns(q), :] = mm(second_bt[q], back[:, columns(q)], NT)
        store(grads, 1, q, diagonal(mm(mixed[columns(q), :], back[:, columns(q)]).T))
    for q in range(pairs):
        pair = regroup(wide, q, 2 * pairs)
        store(grads, 0, q, diagonal(mm(pair, right_act[:, columns(q)])))
        piece = mm(first_bt[q], pair).astype(BF)
        turned[columns(q), :] = piece
        chan_back[:, columns(q)] = mm(right_t[...], piece, NT)
    right_grad[...] = mm(act[...], turned[...]).T


def turn_kernel(
    rows,
    upstream,
    act,
    chan_back,
    act_low,
    left,
    left_t_low,
    second_bt,
    first_bt,
    eye,
    onehot,
    mask,
    input_grad,
    left_grad,
    gate_low,
    back_low,
    mixed_grad,
    sent,
    wide,
    left_acc,
):
    step = pl.program_id(0)
    steps = pl.num_programs(0)
    pairs = second_bt.shape[0]

    gy = upstream[...].astype(F32)
    carried = mm(left[...], rows[...])
    incoming = (gy * carried + chan_back[...]).astype(BF)
    input_grad[...] = incoming
    term = mm((gy * act[...].astype(F32)).astype(BF), rows[...], NT)

    @pl.when(step == 0)
    def _():
        left_acc[...] = term

    @pl.when(step > 0)
    def _():
        left_acc[...] += term

    gate = (incoming.astype(F32) * act_low[...].astype(F32)).astype(BF)
    gate_low[...] = gate
    back = mm(left_t_low[...], gate).astype(BF)
    back_low[...] = back
    for q in range(pairs):
        at = pl.multiple_of((step * pairs + q) * 128, 128)
        wide[pl.ds(at, 128), :] = mm(second_bt[q], back[:, columns(q)], NT)

    @pl.when(step == steps - 1)
    def _():
        for q in range(first_bt.shape[0]):
            pair = regroup(wide, q, 2 * first_bt.shape[0])
            mixed_grad[columns(q), :] = pair
            piece = mm(first_bt[q], pair).astype(BF)
            sent[:, columns(q)] = mm(eye[...], piece, NT).astype(BF)
        left_grad[...] = mm(
            left_acc[...] * mask[...].astype(F32), onehot[...].astype(F32), precision=lax.Precision.HIGHEST
        )


def lower_kernel(
    rows,
    first_bd,
    second_bd,
    left,
    gate,
    back,
    mixed_grad,
    onehot,
    mask,
    carried,
    left_grad,
    grads,
    wide,
    turned,
):
    pairs = first_bd.shape[0]
    for q in range(pairs):
        wide[columns(q), :] = mm(first_bd[q], rows[:, columns(q)], NT)
        store(grads, 0, q, diagonal(mm(mixed_grad[columns(q), :], rows[:, columns(q)])))
    for q in range(pairs):
        pair = regroup(wide, q, 2 * pairs)
        store(grads, 1, q, diagonal(mm(pair, back[:, columns(q)]).T))
        hidden = mm(second_bd[q], pair).astype(BF)
        turned[columns(q), :] = hidden
        carried[:, columns(q)] = mm(left[...], hidden, NT)
    term = mm(gate[...], turned[...])
    left_grad[...] = mm(term * mask[...].astype(F32), onehot[...].astype(F32), precision=lax.Precision.HIGHEST)


def last_kernel(received, right_t, upstream, carried, act, input_grad, right_grad):
    step = pl.program_id(0)
    chan_back = mm(right_t[...], received[...])
    input_grad[...] = (upstream[...].astype(F32) * carried[...] + chan_back).astype(BF)
    term = mm(received[...], act[...], NT)

    @pl.when(step == 0)
    def _():
        right_grad[...] = term

    @pl.when(step > 0)
    def _():
        right_grad[...] += term


def unpack_kernel(sums, first, second):
    side = first.shape[1]
    for part, out in enumerate((first, second)):
        block = sums[:, part].astype(F32).reshape(-1, 2 * side)
        for q in range(out.shape[0] // 2):
            out[2 * q] = block[half(q), :side]
            out[2 * q + 1] = block[half(q), side:]


def swap(value):
    return lax.ppermute(value, "pipe", [(0, 1), (1, 0)])


def after(value, *others):
    return lax.optimization_barrier((value, *others))[0]


def exchange(rows, devices):
    chunks = rows.reshape(devices, rows.shape[0] // devices, *rows.shape[1:])
    return lax.all_to_all(chunks, "blk", split_axis=0, concat_axis=0, tiled=True).reshape(rows.shape)


def summed(parts, devices, others):
    far = 12 if devices == 16 else 0
    members = devices // 2 if far else devices
    groups = [[member ^ f for member in range(members)] for f in ((0, far) if far else (0,))]
    shape = (members, devices // members * parts.shape[1]) + parts.shape[2:]

    def exchanged(value):
        return lax.all_to_all(value, "blk", split_axis=0, concat_axis=0, axis_index_groups=groups, tiled=True)

    pieces = after(exchanged(parts.reshape(shape)), *others)
    total = jnp.sum(pieces.astype(F32), axis=0).astype(BF)
    if far:
        came = lax.ppermute(total, "blk", [(i, i ^ far) for i in range(devices)])
        total = (total.astype(F32) + came.astype(F32)).astype(BF)
    return exchanged(jnp.broadcast_to(total[None], shape)).reshape(parts.shape)


def body(x_saved, cotangent, seq_right, seq_left, chan_first, chan_second):
    devices = lax.axis_size("blk")
    core = lax.axis_index("pipe")
    p = core.astype(jnp.int32).reshape(1)
    saved = x_saved[0]
    micro, tokens, width = saved.shape
    span = seq_right.shape[2]
    per, count = seq_left.shape[1], seq_left.shape[2]
    blocks, side = chan_first.shape[1], chan_first.shape[2]
    pairs = blocks // 2

    sent = lax.dynamic_index_in_dim(saved, 1 - core, 0, keepdims=False)
    received = swap(sent)
    right_own = seq_right[0, 0]
    right_other = swap(right_own)
    first_own, first_other = chan_first[0], swap(chan_first[0])
    second_own, second_other = chan_second[0], swap(chan_second[0])

    place = np.arange(tokens)
    mask = jnp.asarray(place[:, None] // count == place[None, :] % per, BF)
    onehot = jnp.asarray(place[:, None] // per == np.arange(count)[None, :], BF)
    eye = jnp.asarray(np.eye(tokens), BF)

    step = width // 4
    square = whole((tokens, tokens))
    narrow = whole((tokens, count))
    moving = pl.BlockSpec((tokens, step), lambda i, *_: (0, i))
    act_shape = (tokens, width)
    col_shape = (width, tokens)
    pair_shape = (pairs, 2 * side, 2 * side)
    owned = (devices, 2, pairs * side // devices, 2 * side)
    act_full, col_full, pair_full = map(whole, (act_shape, col_shape, pair_shape))
    box = whole((blocks, side, side))
    squared = sds((tokens, tokens), BF)

    full, turned = call(left_kernel, "left", [squared] * 2, (1,), [narrow, narrow, square], [square] * 2, room=8)(
        seq_left[0].reshape(per * count, count), onehot, mask
    )
    full_other, turned_other = swap(full), swap(turned)
    turned_1 = jnp.where(core == 0, turned_other, turned)
    mine = after(core, sent)
    upstream, kept = lax.optimization_barrier(
        tuple(lax.dynamic_index_in_dim(whole_array, mine, 0, keepdims=False) for whole_array in (cotangent, saved))
    )
    act_1 = jnp.where(core == 0, received, kept)
    gate_1 = after((upstream.astype(F32) * act_1.astype(F32)).astype(BF))
    back_1 = jnp.dot(turned_1, gate_1, preferred_element_type=F32).astype(BF)
    returned_1 = exchange(back_1, devices)
    p, received, kept = lax.optimization_barrier((p, received, kept, back_1))[:3]
    act_0, act_1 = jnp.where(core == 0, kept, received), jnp.where(core == 0, received, kept)

    def expand(p, section):
        return call(
            functools.partial(expand_kernel, section),
            "expand",
            [sds(pair_shape, BF)] * 4,
            (1,),
            [box] * 4,
            [pair_full] * 4,
            scalars=1,
        )(p, first_own, first_other, second_own, second_other)

    fbd_1, fbt_1, sbd_1, sbt_1 = expand(p, 1)
    rows_1, mixed_1, right_act_1, right_t_1, right_t_0, right_0 = call(
        forward_kernel,
        "forward",
        [sds(act_shape, BF), sds(col_shape, BF), sds(act_shape, BF)] + [squared] * 3,
        (1,),
        [act_full, square, square, pair_full, pair_full, square],
        [act_full, col_full, act_full] + [square] * 3,
        [pltpu.VMEM(col_shape, F32)],
        scalars=1,
    )(
        p,
        act_1,
        right_own,
        right_other,
        fbd_1,
        sbd_1,
        eye,
    )
    gathered_1 = exchange(rows_1, devices)
    p = after(p, rows_1)
    fbd_0, fbt_0, sbd_0, sbt_0 = expand(p, 0)

    right_act_0, chan_back_1, right_grad_1, grads_1 = call(
        middle_kernel,
        "middle",
        [sds(act_shape, BF), sds(act_shape, F32), sds((span, span), F32), sds(owned, BF)],
        (1,),
        [act_full, pair_full, pair_full, col_full, act_full, square, act_full, square, act_full],
        [act_full, act_full, square, whole(owned)],
        [pltpu.VMEM(col_shape, F32), pltpu.VMEM(col_shape, BF)],
    )(returned_1, sbt_1, fbt_1, mixed_1, right_act_1, right_t_1, act_1, right_0, act_0)
    gathered_0 = exchange(right_act_0, devices)

    input_1, left_grad_1, gate_0, back_0, mixed_grad_0, sent_0 = call(
        turn_kernel,
        "turn",
        [
            sds(act_shape, BF),
            sds((tokens, count), F32),
            sds(act_shape, BF),
            sds(act_shape, BF),
            sds(col_shape, BF),
            sds(act_shape, BF),
        ],
        (width // step,),
        [
            moving,
            moving,
            moving,
            moving,
            moving,
            square,
            square,
            pl.BlockSpec((step // (2 * side), 2 * side, 2 * side), lambda i: (i, 0, 0)),
            pair_full,
            square,
            narrow,
            square,
        ],
        [moving, narrow, moving, moving, col_full, act_full],
        [pltpu.VMEM(col_shape, F32), pltpu.VMEM((tokens, tokens), F32)],
        room=62,
    )(
        gathered_1,
        upstream,
        act_1,
        chan_back_1,
        act_0,
        jnp.where(core == 0, full_other, full),
        jnp.where(core == 0, turned, turned_other),
        sbt_0,
        fbt_0,
        eye,
        onehot,
        mask,
    )
    returned_0 = exchange(sent_0, devices)


    carried_0, left_grad_0, grads_0 = call(
        lower_kernel,
        "lower",
        [sds(act_shape, F32), sds((tokens, count), F32), sds(owned, BF)],
        (1,),
        [act_full, pair_full, pair_full, square, act_full, act_full, col_full, narrow, square],
        [act_full, narrow, whole(owned)],
        [pltpu.VMEM(col_shape, F32), pltpu.VMEM(col_shape, BF)],
    )(gathered_0, fbd_0, sbd_0, jnp.where(core == 0, full, full_other), gate_0, back_0, mixed_grad_0, onehot, mask)

    own = jnp.where(core == 0, grads_0, grads_1).astype(F32)
    parts = (own + swap(jnp.where(core == 0, grads_1, grads_0)).astype(F32)).astype(BF)

    input_0, right_grad_0 = call(
        last_kernel,
        "last",
        [sds(act_shape, BF), sds((span, span), F32)],
        (width // step,),
        [moving, square, moving, moving, moving],
        [moving, square],
    )(returned_0, right_t_0, input_1, carried_0, act_0)

    def to_section(low, high):
        return jnp.where(core == 0, low, high) + swap(jnp.where(core == 0, high, low))

    left_grad = to_section(left_grad_0, left_grad_1).reshape(per, count, count)
    right_grad = to_section(right_grad_0, right_grad_1)
    input_grad = jnp.where(
        core == 0, jnp.stack([input_0, swap(input_0)]), jnp.stack([swap(input_1), input_1])
    )
    sums = summed(after(parts, returned_0), devices, (input_grad, left_grad, right_grad))
    parts = 4
    first_grad, second_grad = call(
        unpack_kernel,
        "unpack",
        [sds((blocks, side, side), F32)] * 2,
        (parts,),
        [pl.BlockSpec((devices // parts,) + owned[1:], lambda i: (i, 0, 0, 0))],
        [pl.BlockSpec((blocks // parts, side, side), lambda i: (i, 0, 0))] * 2,
        room=8,
    )(sums)
    return (
        input_grad[None],
        right_grad[None, None],
        left_grad[None],
        first_grad[None],
        second_grad[None],
    )


def solution(mesh):
    in_specs = (
        P("pipe", None, "blk", None),
        P(None, "blk", None),
        P("pipe", "blk", None, None),
        P("pipe", "blk", None, None),
        P("pipe", None, None, None),
        P("pipe", None, None, None),
    )
    out_specs = (
        P("pipe", None, "blk", None),
        P("pipe", "blk", None, None),
        P("pipe", "blk", None, None),
        P("pipe", None, None, None),
        P("pipe", None, None, None),
    )
    return jax.shard_map(body, mesh=mesh, in_specs=in_specs, out_specs=out_specs, check_vma=False)
```

```python
import functools

import jax
import jax.numpy as jnp
import numpy as np
from jax import lax
from jax.experimental import pallas as pl
from jax.experimental.pallas import tpu as pltpu
from jax.sharding import PartitionSpec as P

BF = jnp.bfloat16
F32 = jnp.float32
NN = (((1,), (0,)), ((), ()))
NT = (((1,), (1,)), ((), ()))


def mm(a, b, dims=NN, precision=None):
    return lax.dot_general(a, b, dims, preferred_element_type=F32, precision=precision)


def whole(shape):
    return pl.BlockSpec(shape, lambda *_: (0,) * len(shape))


def call(kernel, name, out_shape, grid, in_specs, out_specs, scratch=(), scalars=0, room=62):
    params = pltpu.CompilerParams(vmem_limit_bytes=room * 1024 * 1024)
    estimate = pl.CostEstimate(flops=1 << 28, bytes_accessed=8 << 20, transcendentals=0)
    spec = pltpu.PrefetchScalarGridSpec(
        num_scalar_prefetch=scalars, grid=grid, in_specs=in_specs, out_specs=out_specs, scratch_shapes=scratch
    )
    return pl.pallas_call(
        kernel, out_shape=out_shape, grid_spec=spec, compiler_params=params, cost_estimate=estimate, name=name
    )


def sds(shape, dtype):
    return jax.ShapeDtypeStruct(shape, dtype)


def columns(q):
    return slice(128 * q, 128 * (q + 1))


def half(q):
    return slice(64 * q, 64 * (q + 1))


def pick(p, low, high):
    return jnp.where(p[0] == 0, low.astype(F32), high.astype(F32))


def regroup(wide, q, blocks):
    parts = [wide[pl.ds(2 * q + h, blocks, stride=blocks), :] for h in range(2)]
    return jnp.concatenate(parts, axis=0).astype(BF)


def diagonal(product):
    lane = lax.broadcasted_iota(jnp.int32, (64, 128), 1)
    return jnp.where(lane < 64, product[:64], product[64:])


def store(grads, part, q, value):
    rows = grads.shape[2]
    piece = min(rows, 64)
    for first in range(0, 64, piece):
        owner, at = divmod(64 * q + first, rows)
        grads[owner, part, at : at + piece, :] = value[first : first + piece].astype(grads.dtype)


def spread(left, onehot, mask):
    return (mm(left, onehot, NT) * mask.astype(F32)).astype(BF)


def spread_turned(left, onehot, mask):
    return (mm(onehot, left, NT) * mask.astype(F32).T).astype(BF)


def left_kernel(left, onehot, mask, full, turned):
    full[...] = spread(left[...], onehot[...], mask[...])
    turned[...] = spread_turned(left[...], onehot[...], mask[...])


def expand_kernel(section, p, first, first_other, second, second_other, first_bd, first_bt, second_bd, second_bt):
    side = first.shape[1]
    zero = jnp.zeros((side, side), F32)
    for own, other, straight, turned in (
        (first, first_other, first_bd, first_bt),
        (second, second_other, second_bd, second_bt),
    ):
        for q in range(own.shape[0] // 2):
            pair = [(own[2 * q + h], other[2 * q + h]) for h in range(2)]
            parts = [pick(p, b, a) if section else pick(p, a, b) for a, b in pair]
            block = jnp.concatenate(
                [jnp.concatenate([parts[0], zero], axis=1), jnp.concatenate([zero, parts[1]], axis=1)], axis=0
            )
            straight[q] = block.astype(BF)
            turned[q] = block.T.astype(BF)


def forward_kernel(
    p,
    act,
    right_own,
    right_other,
    first_bd,
    second_bd,
    eye,
    order,
    rows,
    mixed,
    right_act,
    right_t_1,
    right_t_0,
    right_0,
    wide,
):
    low = mm(order[...], pick(p, right_own[...], right_other[...]).astype(BF)).astype(BF)
    high = mm(order[...], pick(p, right_other[...], right_own[...]).astype(BF)).astype(BF)
    right_0[...] = low
    right_t_0[...] = low.astype(F32).T.astype(BF)
    right_t_1[...] = high.astype(F32).T.astype(BF)
    right_act[...] = mm(high, act[...]).astype(BF)
    pairs = first_bd.shape[0]
    for q in range(pairs):
        wide[columns(q), :] = mm(first_bd[q], right_act[:, columns(q)], NT)
    for q in range(pairs):
        pair = regroup(wide, q, 2 * pairs)
        mixed[columns(q), :] = pair
        hidden = mm(second_bd[q], pair).astype(BF)
        rows[:, columns(q)] = mm(eye[...], hidden, NT).astype(BF)


def middle_kernel(
    back,
    second_bt,
    first_bt,
    mixed,
    right_act,
    right_t,
    act,
    right_low,
    act_low,
    order,
    right_act_low,
    chan_back,
    right_grad,
    grads,
    wide,
    turned,
):
    right_act_low[...] = mm(right_low[...], act_low[...]).astype(BF)
    pairs = first_bt.shape[0]
    for q in range(pairs):
        wide[columns(q), :] = mm(second_bt[q], back[:, columns(q)], NT)
        store(grads, 1, q, diagonal(mm(mixed[columns(q), :], back[:, columns(q)]).T))
    for q in range(pairs):
        pair = regroup(wide, q, 2 * pairs)
        store(grads, 0, q, diagonal(mm(pair, right_act[:, columns(q)])))
        piece = mm(first_bt[q], pair).astype(BF)
        turned[columns(q), :] = piece
        chan_back[:, columns(q)] = mm(right_t[...], piece, NT)
    right_grad[...] = mm(order[...].astype(F32).T, mm(act[...], turned[...]), NT, lax.Precision.HIGHEST)


def turn_kernel(
    rows,
    upstream,
    act,
    chan_back,
    act_low,
    left,
    left_t_low,
    second_bt,
    first_bt,
    eye,
    onehot,
    mask,
    input_grad,
    left_grad,
    gate_low,
    back_low,
    mixed_grad,
    sent,
    wide,
    left_acc,
):
    step = pl.program_id(0)
    steps = pl.num_programs(0)
    pairs = second_bt.shape[0]

    gy = upstream[...].astype(F32)
    carried = mm(left[...], rows[...])
    incoming = (gy * carried + chan_back[...]).astype(BF)
    input_grad[...] = incoming
    term = mm((gy * act[...].astype(F32)).astype(BF), rows[...], NT)

    @pl.when(step == 0)
    def _():
        left_acc[...] = term

    @pl.when(step > 0)
    def _():
        left_acc[...] += term

    gate = (incoming.astype(F32) * act_low[...].astype(F32)).astype(BF)
    gate_low[...] = gate
    back = mm(left_t_low[...], gate).astype(BF)
    back_low[...] = back
    for q in range(pairs):
        at = pl.multiple_of((step * pairs + q) * 128, 128)
        wide[pl.ds(at, 128), :] = mm(second_bt[q], back[:, columns(q)], NT)

    @pl.when(step == steps - 1)
    def _():
        for q in range(first_bt.shape[0]):
            pair = regroup(wide, q, 2 * first_bt.shape[0])
            mixed_grad[columns(q), :] = pair
            piece = mm(first_bt[q], pair).astype(BF)
            sent[:, columns(q)] = mm(eye[...], piece, NT).astype(BF)
        left_grad[...] = mm(
            left_acc[...] * mask[...].astype(F32), onehot[...].astype(F32), precision=lax.Precision.HIGHEST
        )


def lower_kernel(
    rows,
    first_bd,
    second_bd,
    left,
    gate,
    back,
    mixed_grad,
    onehot,
    mask,
    carried,
    left_grad,
    grads,
    wide,
    turned,
):
    pairs = first_bd.shape[0]
    for q in range(pairs):
        wide[columns(q), :] = mm(first_bd[q], rows[:, columns(q)], NT)
        store(grads, 0, q, diagonal(mm(mixed_grad[columns(q), :], rows[:, columns(q)])))
    for q in range(pairs):
        pair = regroup(wide, q, 2 * pairs)
        store(grads, 1, q, diagonal(mm(pair, back[:, columns(q)]).T))
        hidden = mm(second_bd[q], pair).astype(BF)
        turned[columns(q), :] = hidden
        carried[:, columns(q)] = mm(left[...], hidden, NT)
    term = mm(gate[...], turned[...])
    left_grad[...] = mm(term * mask[...].astype(F32), onehot[...].astype(F32), precision=lax.Precision.HIGHEST)


def last_kernel(received, right_t, order, upstream, carried, act, input_grad, right_grad, right_acc):
    step = pl.program_id(0)
    chan_back = mm(right_t[...], received[...])
    input_grad[...] = (upstream[...].astype(F32) * carried[...] + chan_back).astype(BF)
    term = mm(received[...], act[...], NT)

    @pl.when(step == 0)
    def _():
        right_acc[...] = term

    @pl.when(step > 0)
    def _():
        right_acc[...] += term

    @pl.when(step == pl.num_programs(0) - 1)
    def _():
        right_grad[...] = mm(order[...].astype(F32).T, right_acc[...], precision=lax.Precision.HIGHEST)


def unpack_kernel(sums, first, second):
    side = first.shape[1]
    for part, out in enumerate((first, second)):
        block = sums[:, part].astype(F32).reshape(-1, 2 * side)
        for q in range(out.shape[0] // 2):
            out[2 * q] = block[half(q), :side]
            out[2 * q + 1] = block[half(q), side:]


def swap(value):
    return lax.ppermute(value, "pipe", [(0, 1), (1, 0)])


def after(value, *others):
    return lax.optimization_barrier((value, *others))[0]


def ring(devices):
    return [10, 7, 4, 1, 11, 12, 5, 3, 15, 0, 14, 6, 8, 2, 13, 9] if devices == 16 else list(range(devices))


def exchange(rows, devices):
    chunks = rows.reshape(devices, rows.shape[0] // devices, *rows.shape[1:])
    came = lax.all_to_all(chunks, "blk", split_axis=0, concat_axis=0, axis_index_groups=[ring(devices)], tiled=True)
    return came.reshape(rows.shape)


def summed(parts, devices, others):
    far = 12 if devices == 16 else 0
    members = devices // 2 if far else devices
    groups = [[member ^ f for member in ((3, 5, 0, 4, 1, 6, 7, 2) if far else range(members))] for f in ((0, far) if far else (0,))]
    shape = (members, devices // members * parts.shape[1]) + parts.shape[2:]

    def exchanged(value):
        return lax.all_to_all(value, "blk", split_axis=0, concat_axis=0, axis_index_groups=groups, tiled=True)

    pieces = after(exchanged(parts.reshape(shape)), *others)
    total = jnp.sum(pieces.astype(F32), axis=0).astype(BF)
    if far:
        came = lax.ppermute(total, "blk", [(i, i ^ far) for i in range(devices)])
        total = (total.astype(F32) + came.astype(F32)).astype(BF)
    return exchanged(jnp.broadcast_to(total[None], shape)).reshape(parts.shape)


def body(x_saved, cotangent, seq_right, seq_left, chan_first, chan_second):
    devices = lax.axis_size("blk")
    core = lax.axis_index("pipe")
    p = core.astype(jnp.int32).reshape(1)
    saved = x_saved[0]
    micro, tokens, width = saved.shape
    span = seq_right.shape[2]
    per, count = seq_left.shape[1], seq_left.shape[2]
    blocks, side = chan_first.shape[1], chan_first.shape[2]
    pairs = blocks // 2

    sent = lax.dynamic_index_in_dim(saved, 1 - core, 0, keepdims=False)
    received = swap(sent)
    right_own = seq_right[0, 0]
    right_other = swap(right_own)
    first_own, first_other = chan_first[0], swap(chan_first[0])
    second_own, second_other = chan_second[0], swap(chan_second[0])

    place = np.arange(tokens)
    mask = jnp.asarray(place[:, None] // count == place[None, :] % per, BF)
    whose = np.repeat(ring(devices), per)
    onehot = jnp.asarray(whose[:, None] == np.arange(count)[None, :], BF)
    order = jnp.asarray((whose * per + place % per)[:, None] == place[None, :], BF)
    eye = jnp.asarray(np.eye(tokens), BF)

    step = width // 4
    square = whole((tokens, tokens))
    narrow = whole((tokens, count))
    moving = pl.BlockSpec((tokens, step), lambda i, *_: (0, i))
    act_shape = (tokens, width)
    col_shape = (width, tokens)
    pair_shape = (pairs, 2 * side, 2 * side)
    owned = (devices, 2, pairs * side // devices, 2 * side)
    act_full, col_full, pair_full = map(whole, (act_shape, col_shape, pair_shape))
    box = whole((blocks, side, side))
    squared = sds((tokens, tokens), BF)

    full, turned = call(left_kernel, "left", [squared] * 2, (1,), [narrow, narrow, square], [square] * 2, room=8)(
        seq_left[0].reshape(per * count, count), onehot, mask
    )
    full_other, turned_other = swap(full), swap(turned)
    turned_1 = jnp.where(core == 0, turned_other, turned)
    mine = after(core, sent)
    upstream, kept = lax.optimization_barrier(
        tuple(lax.dynamic_index_in_dim(whole_array, mine, 0, keepdims=False) for whole_array in (cotangent, saved))
    )
    act_1 = jnp.where(core == 0, received, kept)
    gate_1 = after((upstream.astype(F32) * act_1.astype(F32)).astype(BF))
    back_1 = jnp.dot(turned_1, gate_1, preferred_element_type=F32).astype(BF)
    returned_1 = exchange(back_1, devices)
    p, received, kept = lax.optimization_barrier((p, received, kept, back_1))[:3]
    act_0, act_1 = jnp.where(core == 0, kept, received), jnp.where(core == 0, received, kept)

    def expand(p, section):
        return call(
            functools.partial(expand_kernel, section),
            "expand",
            [sds(pair_shape, BF)] * 4,
            (1,),
            [box] * 4,
            [pair_full] * 4,
            scalars=1,
        )(p, first_own, first_other, second_own, second_other)

    fbd_1, fbt_1, sbd_1, sbt_1 = expand(p, 1)
    rows_1, mixed_1, right_act_1, right_t_1, right_t_0, right_0 = call(
        forward_kernel,
        "forward",
        [sds(act_shape, BF), sds(col_shape, BF), sds(act_shape, BF)] + [squared] * 3,
        (1,),
        [act_full, square, square, pair_full, pair_full, square, square],
        [act_full, col_full, act_full] + [square] * 3,
        [pltpu.VMEM(col_shape, F32)],
        scalars=1,
    )(
        p,
        act_1,
        right_own,
        right_other,
        fbd_1,
        sbd_1,
        eye,
        order,
    )
    gathered_1 = exchange(rows_1, devices)
    p = after(p, rows_1)
    fbd_0, fbt_0, sbd_0, sbt_0 = expand(p, 0)

    right_act_0, chan_back_1, right_grad_1, grads_1 = call(
        middle_kernel,
        "middle",
        [sds(act_shape, BF), sds(act_shape, F32), sds((span, span), F32), sds(owned, BF)],
        (1,),
        [act_full, pair_full, pair_full, col_full, act_full, square, act_full, square, act_full, square],
        [act_full, act_full, square, whole(owned)],
        [pltpu.VMEM(col_shape, F32), pltpu.VMEM(col_shape, BF)],
    )(returned_1, sbt_1, fbt_1, mixed_1, right_act_1, right_t_1, act_1, right_0, act_0, order)
    gathered_0 = exchange(right_act_0, devices)

    input_1, left_grad_1, gate_0, back_0, mixed_grad_0, sent_0 = call(
        turn_kernel,
        "turn",
        [
            sds(act_shape, BF),
            sds((tokens, count), F32),
            sds(act_shape, BF),
            sds(act_shape, BF),
            sds(col_shape, BF),
            sds(act_shape, BF),
        ],
        (width // step,),
        [
            moving,
            moving,
            moving,
            moving,
            moving,
            square,
            square,
            pl.BlockSpec((step // (2 * side), 2 * side, 2 * side), lambda i: (i, 0, 0)),
            pair_full,
            square,
            narrow,
            square,
        ],
        [moving, narrow, moving, moving, col_full, act_full],
        [pltpu.VMEM(col_shape, F32), pltpu.VMEM((tokens, tokens), F32)],
        room=62,
    )(
        gathered_1,
        upstream,
        act_1,
        chan_back_1,
        act_0,
        jnp.where(core == 0, full_other, full),
        jnp.where(core == 0, turned, turned_other),
        sbt_0,
        fbt_0,
        eye,
        onehot,
        mask,
    )
    returned_0 = exchange(sent_0, devices)


    carried_0, left_grad_0, grads_0 = call(
        lower_kernel,
        "lower",
        [sds(act_shape, F32), sds((tokens, count), F32), sds(owned, BF)],
        (1,),
        [act_full, pair_full, pair_full, square, act_full, act_full, col_full, narrow, square],
        [act_full, narrow, whole(owned)],
        [pltpu.VMEM(col_shape, F32), pltpu.VMEM(col_shape, BF)],
    )(gathered_0, fbd_0, sbd_0, jnp.where(core == 0, full, full_other), gate_0, back_0, mixed_grad_0, onehot, mask)

    own = jnp.where(core == 0, grads_0, grads_1).astype(F32)
    parts = (own + swap(jnp.where(core == 0, grads_1, grads_0)).astype(F32)).astype(BF)

    input_0, right_grad_0 = call(
        last_kernel,
        "last",
        [sds(act_shape, BF), sds((span, span), F32)],
        (width // step,),
        [moving, square, square, moving, moving, moving],
        [moving, square],
        [pltpu.VMEM((span, span), F32)],
    )(returned_0, right_t_0, order, input_1, carried_0, act_0)

    def to_section(low, high):
        return jnp.where(core == 0, low, high) + swap(jnp.where(core == 0, high, low))

    left_grad = to_section(left_grad_0, left_grad_1).reshape(per, count, count)
    right_grad = to_section(right_grad_0, right_grad_1)
    input_grad = jnp.where(
        core == 0, jnp.stack([input_0, swap(input_0)]), jnp.stack([swap(input_1), input_1])
    )
    sums = summed(after(parts, returned_0), devices, (input_grad, left_grad, right_grad))
    parts = 4
    first_grad, second_grad = call(
        unpack_kernel,
        "unpack",
        [sds((blocks, side, side), F32)] * 2,
        (parts,),
        [pl.BlockSpec((devices // parts,) + owned[1:], lambda i: (i, 0, 0, 0))],
        [pl.BlockSpec((blocks // parts, side, side), lambda i: (i, 0, 0))] * 2,
        room=8,
    )(sums)
    return (
        input_grad[None],
        right_grad[None, None],
        left_grad[None],
        first_grad[None],
        second_grad[None],
    )


def solution(mesh):
    in_specs = (
        P("pipe", None, "blk", None),
        P(None, "blk", None),
        P("pipe", "blk", None, None),
        P("pipe", "blk", None, None),
        P("pipe", None, None, None),
        P("pipe", None, None, None),
    )
    out_specs = (
        P("pipe", None, "blk", None),
        P("pipe", "blk", None, None),
        P("pipe", "blk", None, None),
        P("pipe", None, None, None),
        P("pipe", None, None, None),
    )
    return jax.shard_map(body, mesh=mesh, in_specs=in_specs, out_specs=out_specs, check_vma=False)
```

```python
import functools

import jax
import jax.numpy as jnp
import numpy as np
from jax import lax
from jax.experimental import pallas as pl
from jax.experimental.pallas import tpu as pltpu
from jax.sharding import PartitionSpec as P

BF = jnp.bfloat16
F32 = jnp.float32
NN = (((1,), (0,)), ((), ()))
NT = (((1,), (1,)), ((), ()))


def mm(a, b, dims=NN, precision=None):
    return lax.dot_general(a, b, dims, preferred_element_type=F32, precision=precision)


def whole(shape):
    return pl.BlockSpec(shape, lambda *_: (0,) * len(shape))


def call(kernel, name, out_shape, grid, in_specs, out_specs, scratch=(), scalars=0, room=62):
    params = pltpu.CompilerParams(vmem_limit_bytes=room * 1024 * 1024)
    estimate = pl.CostEstimate(flops=1 << 28, bytes_accessed=8 << 20, transcendentals=0)
    spec = pltpu.PrefetchScalarGridSpec(
        num_scalar_prefetch=scalars, grid=grid, in_specs=in_specs, out_specs=out_specs, scratch_shapes=scratch
    )
    return pl.pallas_call(
        kernel, out_shape=out_shape, grid_spec=spec, compiler_params=params, cost_estimate=estimate, name=name
    )


def sds(shape, dtype):
    return jax.ShapeDtypeStruct(shape, dtype)


def columns(q):
    return slice(128 * q, 128 * (q + 1))


def half(q):
    return slice(64 * q, 64 * (q + 1))


def pick(p, low, high):
    return jnp.where(p[0] == 0, low.astype(F32), high.astype(F32))


def regroup(wide, q, blocks):
    parts = [wide[pl.ds(2 * q + h, blocks, stride=blocks), :] for h in range(2)]
    return jnp.concatenate(parts, axis=0).astype(BF)


def diagonal(product):
    lane = lax.broadcasted_iota(jnp.int32, (64, 128), 1)
    return jnp.where(lane < 64, product[:64], product[64:])


def store(grads, part, q, value):
    rows = grads.shape[2]
    piece = min(rows, 64)
    for first in range(0, 64, piece):
        owner, at = divmod(64 * q + first, rows)
        grads[owner, part, at : at + piece, :] = value[first : first + piece].astype(grads.dtype)


def spread(left, onehot, mask):
    return (mm(left, onehot, NT) * mask.astype(F32)).astype(BF)


def spread_turned(left, onehot, mask):
    return (mm(onehot, left, NT) * mask.astype(F32).T).astype(BF)


def left_kernel(left, onehot, mask, full, turned):
    full[...] = spread(left[...], onehot[...], mask[...])
    turned[...] = spread_turned(left[...], onehot[...], mask[...])


def expand_kernel(section, p, first, first_other, second, second_other, first_bd, first_bt, second_bd, second_bt):
    side = first.shape[1]
    zero = jnp.zeros((side, side), F32)
    for own, other, straight, turned in (
        (first, first_other, first_bd, first_bt),
        (second, second_other, second_bd, second_bt),
    ):
        for q in range(own.shape[0] // 2):
            pair = [(own[2 * q + h], other[2 * q + h]) for h in range(2)]
            parts = [pick(p, b, a) if section else pick(p, a, b) for a, b in pair]
            block = jnp.concatenate(
                [jnp.concatenate([parts[0], zero], axis=1), jnp.concatenate([zero, parts[1]], axis=1)], axis=0
            )
            straight[q] = block.astype(BF)
            turned[q] = block.T.astype(BF)


def forward_kernel(
    p,
    act,
    right_own,
    right_other,
    first_bd,
    second_bd,
    eye,
    order,
    rows,
    mixed,
    right_act,
    right_t_1,
    right_t_0,
    right_0,
    wide,
):
    low = mm(order[...], pick(p, right_own[...], right_other[...]).astype(BF)).astype(BF)
    high = mm(order[...], pick(p, right_other[...], right_own[...]).astype(BF)).astype(BF)
    right_0[...] = low
    right_t_0[...] = low.astype(F32).T.astype(BF)
    right_t_1[...] = high.astype(F32).T.astype(BF)
    right_act[...] = mm(high, act[...]).astype(BF)
    pairs = first_bd.shape[0]
    for q in range(pairs):
        wide[columns(q), :] = mm(first_bd[q], right_act[:, columns(q)], NT)
    for q in range(pairs):
        pair = regroup(wide, q, 2 * pairs)
        mixed[columns(q), :] = pair
        hidden = mm(second_bd[q], pair).astype(BF)
        rows[:, columns(q)] = mm(eye[...], hidden, NT).astype(BF)


def middle_kernel(
    back,
    second_bt,
    first_bt,
    mixed,
    right_act,
    right_t,
    act,
    right_low,
    act_low,
    order,
    right_act_low,
    chan_back,
    right_grad,
    grads,
    wide,
    turned,
):
    right_act_low[...] = mm(right_low[...], act_low[...]).astype(BF)
    pairs = first_bt.shape[0]
    for q in range(pairs):
        wide[columns(q), :] = mm(second_bt[q], back[:, columns(q)], NT)
        store(grads, 1, q, diagonal(mm(mixed[columns(q), :], back[:, columns(q)]).T))
    for q in range(pairs):
        pair = regroup(wide, q, 2 * pairs)
        store(grads, 0, q, diagonal(mm(pair, right_act[:, columns(q)])))
        piece = mm(first_bt[q], pair).astype(BF)
        turned[columns(q), :] = piece
        chan_back[:, columns(q)] = mm(right_t[...], piece, NT)
    right_grad[...] = mm(order[...].astype(F32).T, mm(act[...], turned[...]), NT, lax.Precision.HIGHEST)


def turn_kernel(
    incoming,
    act_low,
    left_t_low,
    second_bt,
    first_bt,
    eye,
    left_term,
    onehot,
    mask,
    left_grad,
    gate_low,
    back_low,
    mixed_grad,
    sent,
    wide,
):
    step = pl.program_id(0)
    pairs = second_bt.shape[0]
    gate = (incoming[...].astype(F32) * act_low[...].astype(F32)).astype(BF)
    gate_low[...] = gate
    back = mm(left_t_low[...], gate).astype(BF)
    back_low[...] = back
    for q in range(pairs):
        at = pl.multiple_of((step * pairs + q) * 128, 128)
        wide[pl.ds(at, 128), :] = mm(second_bt[q], back[:, columns(q)], NT)

    @pl.when(step == pl.num_programs(0) - 1)
    def _():
        for q in range(first_bt.shape[0]):
            pair = regroup(wide, q, 2 * first_bt.shape[0])
            mixed_grad[columns(q), :] = pair
            piece = mm(first_bt[q], pair).astype(BF)
            sent[:, columns(q)] = mm(eye[...], piece, NT).astype(BF)
        left_grad[...] = mm(
            left_term[...] * mask[...].astype(F32), onehot[...].astype(F32), precision=lax.Precision.HIGHEST
        )


def lower_kernel(
    rows,
    first_bd,
    second_bd,
    left,
    gate,
    back,
    mixed_grad,
    onehot,
    mask,
    carried,
    left_grad,
    grads,
    wide,
    turned,
):
    pairs = first_bd.shape[0]
    for q in range(pairs):
        wide[columns(q), :] = mm(first_bd[q], rows[:, columns(q)], NT)
        store(grads, 0, q, diagonal(mm(mixed_grad[columns(q), :], rows[:, columns(q)])))
    for q in range(pairs):
        pair = regroup(wide, q, 2 * pairs)
        store(grads, 1, q, diagonal(mm(pair, back[:, columns(q)]).T))
        hidden = mm(second_bd[q], pair).astype(BF)
        turned[columns(q), :] = hidden
        carried[:, columns(q)] = mm(left[...], hidden, NT)
    term = mm(gate[...], turned[...])
    left_grad[...] = mm(term * mask[...].astype(F32), onehot[...].astype(F32), precision=lax.Precision.HIGHEST)


def last_kernel(received, right_t, order, upstream, carried, act, input_grad, right_grad, right_acc):
    step = pl.program_id(0)
    chan_back = mm(right_t[...], received[...])
    input_grad[...] = (upstream[...].astype(F32) * carried[...] + chan_back).astype(BF)
    term = mm(received[...], act[...], NT)

    @pl.when(step == 0)
    def _():
        right_acc[...] = term

    @pl.when(step > 0)
    def _():
        right_acc[...] += term

    @pl.when(step == pl.num_programs(0) - 1)
    def _():
        right_grad[...] = mm(order[...].astype(F32).T, right_acc[...], precision=lax.Precision.HIGHEST)


def unpack_kernel(sums, first, second):
    side = first.shape[1]
    for part, out in enumerate((first, second)):
        block = sums[:, part].astype(F32).reshape(-1, 2 * side)
        for q in range(out.shape[0] // 2):
            out[2 * q] = block[half(q), :side]
            out[2 * q + 1] = block[half(q), side:]


def swap(value):
    return lax.ppermute(value, "pipe", [(0, 1), (1, 0)])


def after(value, *others):
    return lax.optimization_barrier((value, *others))[0]


def ring(devices):
    return [10, 7, 4, 1, 11, 12, 5, 3, 15, 0, 14, 6, 8, 2, 13, 9] if devices == 16 else list(range(devices))


def exchange(rows, devices):
    chunks = rows.reshape(devices, rows.shape[0] // devices, *rows.shape[1:])
    came = lax.all_to_all(chunks, "blk", split_axis=0, concat_axis=0, axis_index_groups=[ring(devices)], tiled=True)
    return came.reshape(rows.shape)


def summed(parts, devices, others):
    far = 12 if devices == 16 else 0
    members = devices // 2 if far else devices
    groups = [[member ^ f for member in ((3, 5, 0, 4, 1, 6, 7, 2) if far else range(members))] for f in ((0, far) if far else (0,))]
    shape = (members, devices // members * parts.shape[1]) + parts.shape[2:]

    def exchanged(value):
        return lax.all_to_all(value, "blk", split_axis=0, concat_axis=0, axis_index_groups=groups, tiled=True)

    pieces = after(exchanged(parts.reshape(shape)), *others)
    total = jnp.sum(pieces.astype(F32), axis=0).astype(BF)
    if far:
        came = lax.ppermute(total, "blk", [(i, i ^ far) for i in range(devices)])
        total = (total.astype(F32) + came.astype(F32)).astype(BF)
    return exchanged(jnp.broadcast_to(total[None], shape)).reshape(parts.shape)


def body(x_saved, cotangent, seq_right, seq_left, chan_first, chan_second):
    devices = lax.axis_size("blk")
    core = lax.axis_index("pipe")
    p = core.astype(jnp.int32).reshape(1)
    saved = x_saved[0]
    micro, tokens, width = saved.shape
    span = seq_right.shape[2]
    per, count = seq_left.shape[1], seq_left.shape[2]
    blocks, side = chan_first.shape[1], chan_first.shape[2]
    pairs = blocks // 2

    sent = lax.dynamic_index_in_dim(saved, 1 - core, 0, keepdims=False)
    received = swap(sent)
    right_own = seq_right[0, 0]
    right_other = swap(right_own)
    first_own, first_other = chan_first[0], swap(chan_first[0])
    second_own, second_other = chan_second[0], swap(chan_second[0])

    place = np.arange(tokens)
    mask = jnp.asarray(place[:, None] // count == place[None, :] % per, BF)
    whose = np.repeat(ring(devices), per)
    onehot = jnp.asarray(whose[:, None] == np.arange(count)[None, :], BF)
    order = jnp.asarray((whose * per + place % per)[:, None] == place[None, :], BF)
    eye = jnp.asarray(np.eye(tokens), BF)

    step = width // 4
    square = whole((tokens, tokens))
    narrow = whole((tokens, count))
    moving = pl.BlockSpec((tokens, step), lambda i, *_: (0, i))
    act_shape = (tokens, width)
    col_shape = (width, tokens)
    pair_shape = (pairs, 2 * side, 2 * side)
    owned = (devices, 2, pairs * side // devices, 2 * side)
    act_full, col_full, pair_full = map(whole, (act_shape, col_shape, pair_shape))
    box = whole((blocks, side, side))
    squared = sds((tokens, tokens), BF)

    full, turned = call(left_kernel, "left", [squared] * 2, (1,), [narrow, narrow, square], [square] * 2, room=8)(
        seq_left[0].reshape(per * count, count), onehot, mask
    )
    full_other, turned_other = swap(full), swap(turned)
    turned_1 = jnp.where(core == 0, turned_other, turned)
    mine = after(core, sent)
    upstream, kept = lax.optimization_barrier(
        tuple(lax.dynamic_index_in_dim(whole_array, mine, 0, keepdims=False) for whole_array in (cotangent, saved))
    )
    act_1 = jnp.where(core == 0, received, kept)
    gate_1 = after((upstream.astype(F32) * act_1.astype(F32)).astype(BF))
    back_1 = jnp.dot(turned_1, gate_1, preferred_element_type=F32).astype(BF)
    returned_1 = exchange(back_1, devices)
    p, received, kept = lax.optimization_barrier((p, received, kept, back_1))[:3]
    act_0, act_1 = jnp.where(core == 0, kept, received), jnp.where(core == 0, received, kept)

    def expand(p, section):
        return call(
            functools.partial(expand_kernel, section),
            "expand",
            [sds(pair_shape, BF)] * 4,
            (1,),
            [box] * 4,
            [pair_full] * 4,
            scalars=1,
        )(p, first_own, first_other, second_own, second_other)

    fbd_1, fbt_1, sbd_1, sbt_1 = expand(p, 1)
    rows_1, mixed_1, right_act_1, right_t_1, right_t_0, right_0 = call(
        forward_kernel,
        "forward",
        [sds(act_shape, BF), sds(col_shape, BF), sds(act_shape, BF)] + [squared] * 3,
        (1,),
        [act_full, square, square, pair_full, pair_full, square, square],
        [act_full, col_full, act_full] + [square] * 3,
        [pltpu.VMEM(col_shape, F32)],
        scalars=1,
    )(
        p,
        act_1,
        right_own,
        right_other,
        fbd_1,
        sbd_1,
        eye,
        order,
    )
    gathered_1 = exchange(rows_1, devices)
    p = after(p, rows_1)
    fbd_0, fbt_0, sbd_0, sbt_0 = expand(p, 0)

    right_act_0, chan_back_1, right_grad_1, grads_1 = call(
        middle_kernel,
        "middle",
        [sds(act_shape, BF), sds(act_shape, F32), sds((span, span), F32), sds(owned, BF)],
        (1,),
        [act_full, pair_full, pair_full, col_full, act_full, square, act_full, square, act_full, square],
        [act_full, act_full, square, whole(owned)],
        [pltpu.VMEM(col_shape, F32), pltpu.VMEM(col_shape, BF)],
    )(returned_1, sbt_1, fbt_1, mixed_1, right_act_1, right_t_1, act_1, right_0, act_0, order)
    gathered_0 = exchange(after(right_act_0, sbt_0), devices)

    upstream_1 = lax.dynamic_index_in_dim(cotangent, after(core, rows_1), 0, keepdims=False)
    carried_1 = after(jnp.dot(jnp.where(core == 0, full_other, full), gathered_1, preferred_element_type=F32))
    input_1 = (upstream_1.astype(F32) * carried_1 + chan_back_1).astype(BF)
    gate_1 = (upstream_1.astype(F32) * act_1.astype(F32)).astype(BF)
    left_term = lax.dot_general(after(gate_1), gathered_1, NT, preferred_element_type=F32)

    left_grad_1, gate_0, back_0, mixed_grad_0, sent_0 = call(
        turn_kernel,
        "turn",
        [
            sds((tokens, count), F32),
            sds(act_shape, BF),
            sds(act_shape, BF),
            sds(col_shape, BF),
            sds(act_shape, BF),
        ],
        (width // step,),
        [
            moving,
            moving,
            square,
            pl.BlockSpec((step // (2 * side), 2 * side, 2 * side), lambda i: (i, 0, 0)),
            pair_full,
            square,
            square,
            narrow,
            square,
        ],
        [narrow, moving, moving, col_full, act_full],
        [pltpu.VMEM(col_shape, F32)],
    )(
        input_1,
        act_0,
        jnp.where(core == 0, turned, turned_other),
        sbt_0,
        fbt_0,
        eye,
        left_term,
        onehot,
        mask,
    )
    returned_0 = exchange(sent_0, devices)


    carried_0, left_grad_0, grads_0 = call(
        lower_kernel,
        "lower",
        [sds(act_shape, F32), sds((tokens, count), F32), sds(owned, BF)],
        (1,),
        [act_full, pair_full, pair_full, square, act_full, act_full, col_full, narrow, square],
        [act_full, narrow, whole(owned)],
        [pltpu.VMEM(col_shape, F32), pltpu.VMEM(col_shape, BF)],
    )(gathered_0, fbd_0, sbd_0, jnp.where(core == 0, full, full_other), gate_0, back_0, mixed_grad_0, onehot, mask)

    own = jnp.where(core == 0, grads_0, grads_1).astype(F32)
    parts = (own + swap(jnp.where(core == 0, grads_1, grads_0)).astype(F32)).astype(BF)

    input_0, right_grad_0 = call(
        last_kernel,
        "last",
        [sds(act_shape, BF), sds((span, span), F32)],
        (width // step,),
        [moving, square, square, moving, moving, moving],
        [moving, square],
        [pltpu.VMEM((span, span), F32)],
    )(returned_0, right_t_0, order, input_1, carried_0, act_0)

    def to_section(low, high):
        return jnp.where(core == 0, low, high) + swap(jnp.where(core == 0, high, low))

    left_grad = to_section(left_grad_0, left_grad_1).reshape(per, count, count)
    right_grad = to_section(right_grad_0, right_grad_1)
    input_grad = jnp.where(
        core == 0, jnp.stack([input_0, swap(input_0)]), jnp.stack([swap(input_1), input_1])
    )
    sums = summed(after(parts, returned_0), devices, (input_grad, left_grad, right_grad))
    parts = 4
    first_grad, second_grad = call(
        unpack_kernel,
        "unpack",
        [sds((blocks, side, side), F32)] * 2,
        (parts,),
        [pl.BlockSpec((devices // parts,) + owned[1:], lambda i: (i, 0, 0, 0))],
        [pl.BlockSpec((blocks // parts, side, side), lambda i: (i, 0, 0))] * 2,
        room=8,
    )(sums)
    return (
        input_grad[None],
        right_grad[None, None],
        left_grad[None],
        first_grad[None],
        second_grad[None],
    )


def solution(mesh):
    in_specs = (
        P("pipe", None, "blk", None),
        P(None, "blk", None),
        P("pipe", "blk", None, None),
        P("pipe", "blk", None, None),
        P("pipe", None, None, None),
        P("pipe", None, None, None),
    )
    out_specs = (
        P("pipe", None, "blk", None),
        P("pipe", "blk", None, None),
        P("pipe", "blk", None, None),
        P("pipe", None, None, None),
        P("pipe", None, None, None),
    )
    return jax.shard_map(body, mesh=mesh, in_specs=in_specs, out_specs=out_specs, check_vma=False)
```

```python
import functools

import jax
import jax.numpy as jnp
import numpy as np
from jax import lax
from jax.experimental import pallas as pl
from jax.experimental.pallas import tpu as pltpu
from jax.sharding import PartitionSpec as P

BF = jnp.bfloat16
F32 = jnp.float32
NN = (((1,), (0,)), ((), ()))
NT = (((1,), (1,)), ((), ()))


def mm(a, b, dims=NN, precision=None):
    return lax.dot_general(a, b, dims, preferred_element_type=F32, precision=precision)


def whole(shape):
    return pl.BlockSpec(shape, lambda *_: (0,) * len(shape))


def call(kernel, name, out_shape, grid, in_specs, out_specs, scratch=(), scalars=0, room=62):
    params = pltpu.CompilerParams(vmem_limit_bytes=room * 1024 * 1024)
    estimate = pl.CostEstimate(flops=1 << 28, bytes_accessed=8 << 20, transcendentals=0)
    spec = pltpu.PrefetchScalarGridSpec(
        num_scalar_prefetch=scalars, grid=grid, in_specs=in_specs, out_specs=out_specs, scratch_shapes=scratch
    )
    return pl.pallas_call(
        kernel, out_shape=out_shape, grid_spec=spec, compiler_params=params, cost_estimate=estimate, name=name
    )


def sds(shape, dtype):
    return jax.ShapeDtypeStruct(shape, dtype)


def columns(q):
    return slice(128 * q, 128 * (q + 1))


def half(q):
    return slice(64 * q, 64 * (q + 1))


def pick(p, low, high):
    return jnp.where(p[0] == 0, low.astype(F32), high.astype(F32))


def regroup(wide, q, blocks):
    parts = [wide[pl.ds(2 * q + h, blocks, stride=blocks), :] for h in range(2)]
    return jnp.concatenate(parts, axis=0).astype(BF)


def diagonal(product):
    lane = lax.broadcasted_iota(jnp.int32, (64, 128), 1)
    return jnp.where(lane < 64, product[:64], product[64:])


def store(grads, part, q, value):
    rows = grads.shape[2]
    piece = min(rows, 64)
    for first in range(0, 64, piece):
        owner, at = divmod(64 * q + first, rows)
        grads[owner, part, at : at + piece, :] = value[first : first + piece].astype(grads.dtype)


def spread(left, onehot, mask):
    return (mm(left, onehot, NT) * mask.astype(F32)).astype(BF)


def spread_turned(left, onehot, mask):
    return (mm(onehot, left, NT) * mask.astype(F32).T).astype(BF)


def left_kernel(left, onehot, mask, full, turned):
    full[...] = spread(left[...], onehot[...], mask[...])
    turned[...] = spread_turned(left[...], onehot[...], mask[...])


def expand_kernel(section, p, first, first_other, second, second_other, first_bd, first_bt, second_bd, second_bt):
    side = first.shape[1]
    zero = jnp.zeros((side, side), F32)
    for own, other, straight, turned in (
        (first, first_other, first_bd, first_bt),
        (second, second_other, second_bd, second_bt),
    ):
        for q in range(own.shape[0] // 2):
            pair = [(own[2 * q + h], other[2 * q + h]) for h in range(2)]
            parts = [pick(p, b, a) if section else pick(p, a, b) for a, b in pair]
            block = jnp.concatenate(
                [jnp.concatenate([parts[0], zero], axis=1), jnp.concatenate([zero, parts[1]], axis=1)], axis=0
            )
            straight[q] = block.astype(BF)
            turned[q] = block.T.astype(BF)


def forward_kernel(
    p,
    act,
    right_own,
    right_other,
    first_bd,
    second_bd,
    eye,
    order,
    rows,
    mixed,
    right_act,
    right_t_1,
    right_t_0,
    right_0,
    wide,
):
    low = mm(order[...], pick(p, right_own[...], right_other[...]).astype(BF)).astype(BF)
    high = mm(order[...], pick(p, right_other[...], right_own[...]).astype(BF)).astype(BF)
    right_0[...] = low
    right_t_0[...] = low.astype(F32).T.astype(BF)
    right_t_1[...] = high.astype(F32).T.astype(BF)
    right_act[...] = mm(high, act[...]).astype(BF)
    pairs = first_bd.shape[0]
    for q in range(pairs):
        wide[columns(q), :] = mm(first_bd[q], right_act[:, columns(q)], NT)
    for q in range(pairs):
        pair = regroup(wide, q, 2 * pairs)
        mixed[columns(q), :] = pair
        hidden = mm(second_bd[q], pair).astype(BF)
        rows[:, columns(q)] = mm(eye[...], hidden, NT).astype(BF)


def middle_kernel(
    back,
    second_bt,
    first_bt,
    mixed,
    right_act,
    right_t,
    act,
    right_low,
    act_low,
    order,
    right_act_low,
    chan_back,
    right_grad,
    grads,
    wide,
    turned,
):
    right_act_low[...] = mm(right_low[...], act_low[...]).astype(BF)
    pairs = first_bt.shape[0]
    for q in range(pairs):
        wide[columns(q), :] = mm(second_bt[q], back[:, columns(q)], NT)
        store(grads, 1, q, diagonal(mm(mixed[columns(q), :], back[:, columns(q)]).T))
    for q in range(pairs):
        pair = regroup(wide, q, 2 * pairs)
        store(grads, 0, q, diagonal(mm(pair, right_act[:, columns(q)])))
        piece = mm(first_bt[q], pair).astype(BF)
        turned[columns(q), :] = piece
        chan_back[:, columns(q)] = mm(right_t[...], piece, NT)
    right_grad[...] = mm(order[...].astype(F32).T, mm(act[...], turned[...]), NT, lax.Precision.HIGHEST)


def turn_kernel(
    incoming,
    act_low,
    left_t_low,
    second_bt,
    first_bt,
    eye,
    left_term,
    onehot,
    mask,
    left_grad,
    gate_low,
    back_low,
    mixed_grad,
    sent,
    wide,
):
    step = pl.program_id(0)
    pairs = second_bt.shape[0]
    gate = (incoming[...].astype(F32) * act_low[...].astype(F32)).astype(BF)
    gate_low[...] = gate
    back = mm(left_t_low[...], gate).astype(BF)
    back_low[...] = back
    for q in range(pairs):
        at = pl.multiple_of((step * pairs + q) * 128, 128)
        wide[pl.ds(at, 128), :] = mm(second_bt[q], back[:, columns(q)], NT)

    @pl.when(step == pl.num_programs(0) - 1)
    def _():
        for q in range(first_bt.shape[0]):
            pair = regroup(wide, q, 2 * first_bt.shape[0])
            mixed_grad[columns(q), :] = pair
            piece = mm(first_bt[q], pair).astype(BF)
            sent[:, columns(q)] = mm(eye[...], piece, NT).astype(BF)
        left_grad[...] = mm(
            left_term[...] * mask[...].astype(F32), onehot[...].astype(F32), precision=lax.Precision.HIGHEST
        )


def lower_kernel(
    rows,
    first_bd,
    second_bd,
    left,
    gate,
    back,
    mixed_grad,
    onehot,
    mask,
    carried,
    left_grad,
    grads,
    wide,
    turned,
):
    pairs = first_bd.shape[0]
    for q in range(pairs):
        wide[columns(q), :] = mm(first_bd[q], rows[:, columns(q)], NT)
        store(grads, 0, q, diagonal(mm(mixed_grad[columns(q), :], rows[:, columns(q)])))
    for q in range(pairs):
        pair = regroup(wide, q, 2 * pairs)
        store(grads, 1, q, diagonal(mm(pair, back[:, columns(q)]).T))
        hidden = mm(second_bd[q], pair).astype(BF)
        turned[columns(q), :] = hidden
        carried[:, columns(q)] = mm(left[...], hidden, NT)
    term = mm(gate[...], turned[...])
    left_grad[...] = mm(term * mask[...].astype(F32), onehot[...].astype(F32), precision=lax.Precision.HIGHEST)


def last_kernel(received, right_t, order, upstream, carried, act, input_grad, right_grad, right_acc):
    step = pl.program_id(0)
    chan_back = mm(right_t[...], received[...])
    input_grad[...] = (upstream[...].astype(F32) * carried[...] + chan_back).astype(BF)
    term = mm(received[...], act[...], NT)

    @pl.when(step == 0)
    def _():
        right_acc[...] = term

    @pl.when(step > 0)
    def _():
        right_acc[...] += term

    @pl.when(step == pl.num_programs(0) - 1)
    def _():
        right_grad[...] = mm(order[...].astype(F32).T, right_acc[...], precision=lax.Precision.HIGHEST)


def unpack_kernel(sums, first, second):
    side = first.shape[1]
    for part, out in enumerate((first, second)):
        block = sums[:, part].astype(F32).reshape(-1, 2 * side)
        for q in range(out.shape[0] // 2):
            out[2 * q] = block[half(q), :side]
            out[2 * q + 1] = block[half(q), side:]


def swap(value):
    return lax.ppermute(value, "pipe", [(0, 1), (1, 0)])


def after(value, *others):
    return lax.optimization_barrier((value, *others))[0]


def ring(devices):
    return [10, 7, 4, 1, 11, 12, 5, 3, 15, 0, 14, 6, 8, 2, 13, 9] if devices == 16 else list(range(devices))


def exchange(rows, devices):
    chunks = rows.reshape(devices, rows.shape[0] // devices, *rows.shape[1:])
    came = lax.all_to_all(chunks, "blk", split_axis=0, concat_axis=0, axis_index_groups=[ring(devices)], tiled=True)
    return came.reshape(rows.shape)


def summed(parts, devices, others):
    far = 12 if devices == 16 else 0
    members = devices // 2 if far else devices
    groups = [[member ^ f for member in ((0, 4, 6, 2, 3, 7, 5, 1) if far else range(members))] for f in ((0, far) if far else (0,))]
    shape = (members, devices // members * parts.shape[1]) + parts.shape[2:]

    def exchanged(value):
        return lax.all_to_all(value, "blk", split_axis=0, concat_axis=0, axis_index_groups=groups, tiled=True)

    pieces = after(exchanged(parts.reshape(shape)), *others)
    total = jnp.sum(pieces.astype(F32), axis=0).astype(BF)
    if far:
        came = lax.ppermute(total, "blk", [(i, i ^ far) for i in range(devices)])
        total = (total.astype(F32) + came.astype(F32)).astype(BF)
    return exchanged(jnp.broadcast_to(total[None], shape)).reshape(parts.shape)


def body(x_saved, cotangent, seq_right, seq_left, chan_first, chan_second):
    devices = lax.axis_size("blk")
    core = lax.axis_index("pipe")
    p = core.astype(jnp.int32).reshape(1)
    saved = x_saved[0]
    micro, tokens, width = saved.shape
    span = seq_right.shape[2]
    per, count = seq_left.shape[1], seq_left.shape[2]
    blocks, side = chan_first.shape[1], chan_first.shape[2]
    pairs = blocks // 2

    sent = lax.dynamic_index_in_dim(saved, 1 - core, 0, keepdims=False)
    received = swap(sent)
    right_own = seq_right[0, 0]
    right_other = swap(right_own)
    first_own, first_other = chan_first[0], swap(chan_first[0])
    second_own, second_other = chan_second[0], swap(chan_second[0])

    place = np.arange(tokens)
    mask = jnp.asarray(place[:, None] // count == place[None, :] % per, BF)
    whose = np.repeat(ring(devices), per)
    onehot = jnp.asarray(whose[:, None] == np.arange(count)[None, :], BF)
    order = jnp.asarray((whose * per + place % per)[:, None] == place[None, :], BF)
    eye = jnp.asarray(np.eye(tokens), BF)

    step = width // 4
    square = whole((tokens, tokens))
    narrow = whole((tokens, count))
    moving = pl.BlockSpec((tokens, step), lambda i, *_: (0, i))
    act_shape = (tokens, width)
    col_shape = (width, tokens)
    pair_shape = (pairs, 2 * side, 2 * side)
    owned = (devices, 2, pairs * side // devices, 2 * side)
    act_full, col_full, pair_full = map(whole, (act_shape, col_shape, pair_shape))
    box = whole((blocks, side, side))
    squared = sds((tokens, tokens), BF)

    full, turned = call(left_kernel, "left", [squared] * 2, (1,), [narrow, narrow, square], [square] * 2, room=8)(
        seq_left[0].reshape(per * count, count), onehot, mask
    )
    full_other, turned_other = swap(full), swap(turned)
    turned_1 = jnp.where(core == 0, turned_other, turned)
    mine = after(core, sent)
    upstream, kept = lax.optimization_barrier(
        tuple(lax.dynamic_index_in_dim(whole_array, mine, 0, keepdims=False) for whole_array in (cotangent, saved))
    )
    act_1 = jnp.where(core == 0, received, kept)
    gate_1 = after((upstream.astype(F32) * act_1.astype(F32)).astype(BF))
    back_1 = jnp.dot(turned_1, gate_1, preferred_element_type=F32).astype(BF)
    returned_1 = exchange(back_1, devices)
    p, received, kept = lax.optimization_barrier((p, received, kept, back_1))[:3]
    act_0, act_1 = jnp.where(core == 0, kept, received), jnp.where(core == 0, received, kept)

    def expand(p, section):
        return call(
            functools.partial(expand_kernel, section),
            "expand",
            [sds(pair_shape, BF)] * 4,
            (1,),
            [box] * 4,
            [pair_full] * 4,
            scalars=1,
        )(p, first_own, first_other, second_own, second_other)

    fbd_1, fbt_1, sbd_1, sbt_1 = expand(p, 1)
    rows_1, mixed_1, right_act_1, right_t_1, right_t_0, right_0 = call(
        forward_kernel,
        "forward",
        [sds(act_shape, BF), sds(col_shape, BF), sds(act_shape, BF)] + [squared] * 3,
        (1,),
        [act_full, square, square, pair_full, pair_full, square, square],
        [act_full, col_full, act_full] + [square] * 3,
        [pltpu.VMEM(col_shape, F32)],
        scalars=1,
    )(
        p,
        act_1,
        right_own,
        right_other,
        fbd_1,
        sbd_1,
        eye,
        order,
    )
    gathered_1 = exchange(rows_1, devices)
    p = after(p, rows_1)
    fbd_0, fbt_0, sbd_0, sbt_0 = expand(p, 0)

    right_act_0, chan_back_1, right_grad_1, grads_1 = call(
        middle_kernel,
        "middle",
        [sds(act_shape, BF), sds(act_shape, F32), sds((span, span), F32), sds(owned, BF)],
        (1,),
        [act_full, pair_full, pair_full, col_full, act_full, square, act_full, square, act_full, square],
        [act_full, act_full, square, whole(owned)],
        [pltpu.VMEM(col_shape, F32), pltpu.VMEM(col_shape, BF)],
    )(returned_1, sbt_1, fbt_1, mixed_1, right_act_1, right_t_1, act_1, right_0, act_0, order)
    gathered_0 = exchange(after(right_act_0, sbt_0), devices)

    upstream_1 = lax.dynamic_index_in_dim(cotangent, after(core, rows_1), 0, keepdims=False)
    carried_1 = after(jnp.dot(jnp.where(core == 0, full_other, full), gathered_1, preferred_element_type=F32))
    input_1 = (upstream_1.astype(F32) * carried_1 + chan_back_1).astype(BF)
    gate_1 = (upstream_1.astype(F32) * act_1.astype(F32)).astype(BF)
    left_term = lax.dot_general(after(gate_1), gathered_1, NT, preferred_element_type=F32)

    left_grad_1, gate_0, back_0, mixed_grad_0, sent_0 = call(
        turn_kernel,
        "turn",
        [
            sds((tokens, count), F32),
            sds(act_shape, BF),
            sds(act_shape, BF),
            sds(col_shape, BF),
            sds(act_shape, BF),
        ],
        (width // step,),
        [
            moving,
            moving,
            square,
            pl.BlockSpec((step // (2 * side), 2 * side, 2 * side), lambda i: (i, 0, 0)),
            pair_full,
            square,
            square,
            narrow,
            square,
        ],
        [narrow, moving, moving, col_full, act_full],
        [pltpu.VMEM(col_shape, F32)],
    )(
        input_1,
        act_0,
        jnp.where(core == 0, turned, turned_other),
        sbt_0,
        fbt_0,
        eye,
        left_term,
        onehot,
        mask,
    )
    returned_0 = exchange(sent_0, devices)


    carried_0, left_grad_0, grads_0 = call(
        lower_kernel,
        "lower",
        [sds(act_shape, F32), sds((tokens, count), F32), sds(owned, BF)],
        (1,),
        [act_full, pair_full, pair_full, square, act_full, act_full, col_full, narrow, square],
        [act_full, narrow, whole(owned)],
        [pltpu.VMEM(col_shape, F32), pltpu.VMEM(col_shape, BF)],
    )(gathered_0, fbd_0, sbd_0, jnp.where(core == 0, full, full_other), gate_0, back_0, mixed_grad_0, onehot, mask)

    own = jnp.where(core == 0, grads_0, grads_1).astype(F32)
    parts = (own + swap(jnp.where(core == 0, grads_1, grads_0)).astype(F32)).astype(BF)

    input_0, right_grad_0 = call(
        last_kernel,
        "last",
        [sds(act_shape, BF), sds((span, span), F32)],
        (width // step,),
        [moving, square, square, moving, moving, moving],
        [moving, square],
        [pltpu.VMEM((span, span), F32)],
    )(returned_0, right_t_0, order, input_1, carried_0, act_0)

    def to_section(low, high):
        return jnp.where(core == 0, low, high) + swap(jnp.where(core == 0, high, low))

    left_grad = to_section(left_grad_0, left_grad_1).reshape(per, count, count)
    right_grad = to_section(right_grad_0, right_grad_1)
    input_grad = jnp.where(
        core == 0, jnp.stack([input_0, swap(input_0)]), jnp.stack([swap(input_1), input_1])
    )
    sums = summed(after(parts, returned_0), devices, (input_grad, left_grad, right_grad))
    parts = 4
    first_grad, second_grad = call(
        unpack_kernel,
        "unpack",
        [sds((blocks, side, side), F32)] * 2,
        (parts,),
        [pl.BlockSpec((devices // parts,) + owned[1:], lambda i: (i, 0, 0, 0))],
        [pl.BlockSpec((blocks // parts, side, side), lambda i: (i, 0, 0))] * 2,
        room=8,
    )(sums)
    return (
        input_grad[None],
        right_grad[None, None],
        left_grad[None],
        first_grad[None],
        second_grad[None],
    )


def solution(mesh):
    in_specs = (
        P("pipe", None, "blk", None),
        P(None, "blk", None),
        P("pipe", "blk", None, None),
        P("pipe", "blk", None, None),
        P("pipe", None, None, None),
        P("pipe", None, None, None),
    )
    out_specs = (
        P("pipe", None, "blk", None),
        P("pipe", "blk", None, None),
        P("pipe", "blk", None, None),
        P("pipe", None, None, None),
        P("pipe", None, None, None),
    )
    return jax.shard_map(body, mesh=mesh, in_specs=in_specs, out_specs=out_specs, check_vma=False)
```
